128 devices in a mesh: side: 2 (over core), wide: 16 (over z, y), narrow: 4 (over x).
Axes of the slice: x: 4, y: 4, z: 4, core: 2. Of those that a mesh axis runs over, the one named last changes fastest.
Arguments:
- queries: bfloat16 [64, 8192], P(('side', 'wide')), may hold values from -20 to 20
- key_cache: bfloat16 [64, 4096, 1024], P(('side', 'wide'), 'narrow'), may hold values from -20 to 20
- value_cache: bfloat16 [64, 4096, 1024], P(('side', 'wide'), 'narrow'), may hold values from -6 to 6
- latest_key: bfloat16 [64, 1024], P(('side', 'wide')), may hold values from -20 to 20
- latest_value: bfloat16 [64, 1024], P(('side', 'wide')), may hold values from -6 to 6
- lengths: int32 [64], P(('side', 'wide')), may hold values from 1 to 4096, 131072 in all
- residual: bfloat16 [64, 8192], P(None, ('side', 'wide', 'narrow')), may hold values from -6 to 6
- o_weight: bfloat16 [8192, 8192], P(None, ('side', 'wide', 'narrow')), may hold values from -0.0625 to 0.0625
- norm_gain: bfloat16 [8192], P(('side', 'wide', 'narrow')), may hold values from 0.5 to 1.5
- gate_weight: bfloat16 [8192, 28672], P(None, ('side', 'wide', 'narrow')), may hold values from -0.0625 to 0.0625
- up_weight: bfloat16 [8192, 28672], P(None, ('side', 'wide', 'narrow')), may hold values from -0.0625 to 0.0625
- down_weight: bfloat16 [28672, 8192], P(('side', 'wide', 'narrow')), may hold values from -0.125 to 0.125
Outputs:
- layer_out: bfloat16 [64, 8192], P(None, ('side', 'wide', 'narrow'))
The draws below stay inside these ranges and needn't reach their ends.
Inputs may be any that keep to these rules, and one draw needn't show every extreme that they name: `lengths`: some session has exactly 4096 valid positions.
All inputs are finite; a program needn't handle non-finite values. No bound on the sum of `lengths` on one device may be relied on, other than what follows from the above.
Results may differ from the reference program's by a relative error of at most 0.0152.
Values may be sent and summed in bfloat16 or wider, within the bound.
A program may use at most 64 MiB of HBM per device.

```python
import math
import jax
import jax.numpy as jnp
import numpy as np
from jax import lax

D = 8192
FF = 28672
QUERY_HEADS = 64
KEY_VALUE_HEADS = 8
HEAD_SIZE = 128
QUERY_WIDTH = 8192
SESSION_COUNT = 64
CONTEXT_SLOTS = 4096


def shared_base(key, low_target, high_target):
    leading, second = jax.random.split(jax.random.fold_in(key, 7))
    direction = jnp.where(jax.random.bernoulli(leading, 0.5, (SESSION_COUNT, KEY_VALUE_HEADS, HEAD_SIZE)), 1.0, -1.0).astype(jnp.float32)
    target = jax.random.uniform(second, (SESSION_COUNT,), jnp.float32, low_target, high_target)
    magnitude = jnp.sqrt(target / HEAD_SIZE ** 0.5)
    chosen = jnp.arange(SESSION_COUNT) % 8 == 0
    return (direction, target, magnitude, chosen)


def pick_range():
    return (120.0, 400.0)


def draw_queries(key, part):
    low_target, high_target = pick_range()
    direction, target, magnitude, chosen = shared_base(key, low_target, high_target)
    key = jax.random.fold_in(key, 11)
    unshifted = jnp.clip(jax.random.normal(key, (SESSION_COUNT, QUERY_WIDTH), jnp.float32), -4.0, 4.0)
    lined_up = jnp.broadcast_to(magnitude[:, None, None, None] * direction[:, :, None, :], (SESSION_COUNT, KEY_VALUE_HEADS, QUERY_HEADS // KEY_VALUE_HEADS, HEAD_SIZE)).reshape(SESSION_COUNT, QUERY_WIDTH)
    unshifted = jnp.where(chosen[:, None], lined_up, unshifted)
    return unshifted.astype(jnp.bfloat16)


def draw_key_cache(key, part):
    low_target, high_target = pick_range()
    direction, target, magnitude, chosen = shared_base(key, low_target, high_target)
    key = jax.random.fold_in(key, 13)
    unshifted = jnp.clip(jax.random.normal(key, (SESSION_COUNT, CONTEXT_SLOTS, KEY_VALUE_HEADS * HEAD_SIZE), jnp.float32), -4.0, 4.0)
    leading_row = (magnitude[:, None, None] * direction).reshape(SESSION_COUNT, KEY_VALUE_HEADS * HEAD_SIZE)
    unshifted = unshifted.at[:, 0, :].set(jnp.where(chosen[:, None], leading_row, unshifted[:, 0, :]))
    return unshifted.astype(jnp.bfloat16)


def draw_latest_key(key, part):
    low_target, high_target = pick_range()
    direction, target, magnitude, chosen = shared_base(key, low_target, high_target)
    key = jax.random.fold_in(key, 17)
    unshifted = jnp.clip(jax.random.normal(key, (SESSION_COUNT, KEY_VALUE_HEADS * HEAD_SIZE), jnp.float32), -4.0, 4.0)
    stretch = 1.0 + 2.0 / target
    shifted = ((magnitude * stretch)[:, None, None] * direction).reshape(SESSION_COUNT, KEY_VALUE_HEADS * HEAD_SIZE)
    unshifted = jnp.where(chosen[:, None], shifted, unshifted)
    return unshifted.astype(jnp.bfloat16)


def raised(entries, stream_key, source, target, blocks, factor):
    def block_of(position):
        return (jnp.arange(entries.shape[position]) // (entries.shape[position] // blocks)).reshape((-1,) + (1,) * (entries.ndim - 1 - position))

    one_side = jax.random.permutation(stream_key, blocks)[block_of(target)]
    second = (block_of(target) + blocks // 2) % blocks
    return jnp.where((block_of(source) == one_side) | (block_of(source) == second), factor * entries, entries)


def block_scale(key, dims, shards, low, high):
    loudness = 1.0
    for axis_at, shards_of in shards:
        draws = jax.random.uniform(jax.random.fold_in(jax.random.fold_in(key, 6), axis_at), (shards_of,), jnp.float32, low / len(shards), high / len(shards))
        loudness = loudness * jnp.repeat(jnp.exp(draws), dims[axis_at] // shards_of).reshape((-1,) + (1,) * (len(dims) - 1 - axis_at))
    return loudness


def split_up(number_of, total, bound, lean):
    loads = [(1 << 20) // math.isqrt(grade ** lean) + 1 for grade in range(2, number_of + 1)]
    spare, counts = total - bound - (number_of - 1), [1] * (number_of - 1)
    while spare > 0:
        candidates = [i for i in range(number_of - 1) if counts[i] < bound]
        pool, left = sum([loads[i] for i in candidates]), spare
        for i in candidates:
            more = min(bound - counts[i], max(1, left * loads[i] // pool), spare)
            counts[i] = counts[i] + more
            spare = spare - more
    return np.array([bound] + counts)


def uneven(rng, count, total, reach, slope):
    if count == 2:
        one = jax.random.randint(rng, (), max(1, total - reach), min(reach, total - 1) + 1)
        return jnp.stack([one, total - one])
    sizes = jnp.asarray(split_up(count, total, reach, slope), jnp.int32)
    couples = (count - 1) // 2
    donor, sink = sizes[1:1 + 2 * couples:2], sizes[2:2 + 2 * couples:2]
    room = jnp.minimum(donor - 1, reach - sink)
    passed = jax.random.randint(jax.random.fold_in(rng, 1), (couples,), 0, 1 << 20) % (room + 1)
    sizes = sizes.at[1:1 + 2 * couples:2].set(donor - passed).at[2:2 + 2 * couples:2].set(sink + passed)
    return sizes[jax.random.permutation(jax.random.fold_in(rng, 2), count)]


def normal_values(rng, extent, width, bound, cuts=(), kind=jnp.bfloat16):
    values = width * jax.random.normal(rng, extent, jnp.float32)
    if cuts:
        values = values * block_scale(rng, extent, cuts, -0.22, 0.18)
    return jnp.clip(values, -bound, bound).astype(kind)


def gaussian_with(own_key, shape, scale, reach, cuts, heavy, kind=jnp.bfloat16):
    drawn = scale * jax.random.normal(own_key, shape, jnp.float32)
    if cuts:
        drawn = drawn * block_scale(own_key, shape, cuts, -0.22, 0.18)
    return jnp.clip(raised(drawn, jax.random.fold_in(own_key, 3), *heavy), -reach, reach).astype(kind)


def setup_inputs(seed: int = 0) -> dict:
    key_list = jax.random.split(jax.random.key(seed), 13)
    queries = draw_queries(jax.random.fold_in(key_list[12], 71), 0)
    key_cache = draw_key_cache(jax.random.fold_in(key_list[12], 71), 0)
    value_cache = normal_values(key_list[2], (SESSION_COUNT, CONTEXT_SLOTS, KEY_VALUE_HEADS * HEAD_SIZE), 1.0, 6.0, ((0, 32), (1, 4)))
    latest_key = draw_latest_key(jax.random.fold_in(key_list[12], 71), 0)
    latest_value = normal_values(key_list[4], (SESSION_COUNT, KEY_VALUE_HEADS * HEAD_SIZE), 1.0, 6.0, ((0, 32),))
    lengths = uneven(key_list[5], SESSION_COUNT, SESSION_COUNT * CONTEXT_SLOTS // 2, CONTEXT_SLOTS, 2).astype(jnp.int32)
    residual = normal_values(key_list[6], (SESSION_COUNT, D), 1.0, 6.0, ((1, 128),))
    o_weight = normal_values(key_list[7], (QUERY_WIDTH, D), QUERY_WIDTH ** -0.5, 0.0625, ((1, 128),))
    norm_gain = jnp.clip(1.0 + 0.1 * jax.random.normal(key_list[8], (D,), jnp.float32), 0.5, 1.5).astype(jnp.bfloat16)
    gate_weight = normal_values(key_list[9], (D, FF), D ** -0.5, 0.0625, ((1, 128),))
    up_weight = normal_values(key_list[10], (D, FF), D ** -0.5, 0.0625, ((1, 128),))
    down_weight = gaussian_with(key_list[11], (FF, D), FF ** -0.5, 0.125, ((0, 128),), (0, 1, 128, 5.5))
    return dict(queries=queries, key_cache=key_cache, value_cache=value_cache, latest_key=latest_key, latest_value=latest_value, lengths=lengths, residual=residual, o_weight=o_weight, norm_gain=norm_gain, gate_weight=gate_weight, up_weight=up_weight, down_weight=down_weight)


def reference(queries, key_cache, value_cache, latest_key, latest_value, lengths, residual, o_weight, norm_gain, gate_weight, up_weight, down_weight):
    scaling = HEAD_SIZE ** (-0.5)
    query_groups = QUERY_HEADS // KEY_VALUE_HEADS
    query_lines = queries.astype(jnp.float32).reshape(SESSION_COUNT, KEY_VALUE_HEADS, query_groups, HEAD_SIZE)

    def per_session(items):
        query_one, single_key, single_value, key_incoming, value_incoming, length_one = items
        key_lines = single_key.astype(jnp.float32).reshape(CONTEXT_SLOTS, KEY_VALUE_HEADS, HEAD_SIZE)
        value_lines = single_value.astype(jnp.float32).reshape(CONTEXT_SLOTS, KEY_VALUE_HEADS, HEAD_SIZE)
        scores = jnp.einsum('gqd,tgd->gqt', query_one, key_lines) * scaling
        valid = jnp.arange(CONTEXT_SLOTS, dtype=jnp.int32) < length_one
        scores = jnp.where(valid[None, None, :], scores, jnp.float32(-1e+30))
        largest = lax.optimization_barrier(jnp.max(scores, axis=-1))
        weights = jnp.where(valid[None, None, :], jnp.exp(scores - largest[..., None]), jnp.float32(0.0))
        denominator = lax.optimization_barrier(jnp.sum(weights, axis=-1))
        rounded = lax.optimization_barrier(weights.astype(jnp.bfloat16)).astype(jnp.float32)
        numerator = jnp.einsum('gqt,tgd->gqd', rounded, value_lines)
        incoming_key = key_incoming.astype(jnp.float32).reshape(KEY_VALUE_HEADS, HEAD_SIZE)
        incoming_value = value_incoming.astype(jnp.float32).reshape(KEY_VALUE_HEADS, 1, HEAD_SIZE)
        new_score = jnp.einsum('gqd,gd->gq', query_one, incoming_key) * scaling
        peak = jnp.maximum(largest, new_score)
        shrink = jnp.exp(largest - peak)
        own = jnp.exp(new_score - peak)
        result = (numerator * shrink[..., None] + own[..., None] * incoming_value) / (denominator * shrink + own)[..., None]
        return result.reshape(QUERY_WIDTH).astype(jnp.bfloat16)
    attended = lax.map(per_session, (query_lines, key_cache, value_cache, latest_key, latest_value, lengths))
    projected = jnp.dot(attended, o_weight, preferred_element_type=jnp.float32)
    stream = (residual.astype(jnp.float32) + projected).astype(jnp.bfloat16)
    stream_f = stream.astype(jnp.float32)
    mean_square = lax.optimization_barrier(jnp.mean(stream_f * stream_f, axis=-1, keepdims=True))
    normed = (stream_f * lax.rsqrt(mean_square + 1e-05) * norm_gain.astype(jnp.float32)).astype(jnp.bfloat16)
    gate_sum = jnp.dot(normed, gate_weight, preferred_element_type=jnp.float32)
    up_sum = jnp.dot(normed, up_weight, preferred_element_type=jnp.float32)
    hidden = (jax.nn.silu(gate_sum) * up_sum).astype(jnp.bfloat16)
    down_terms = jnp.dot(hidden, down_weight, preferred_element_type=jnp.float32)
    return (stream_f + down_terms).astype(jnp.bfloat16)
```

```python
import jax
import jax.numpy as jnp
from jax import lax
from jax.experimental import pallas as pl
from jax.experimental.pallas import tpu as pltpu
from jax.sharding import PartitionSpec as P

D = 8192
HEAD = 128
SPAN = 1024
UNITS = 224
SCALE = HEAD**-0.5
NEG = -1e30
MESH = pl.DeviceIdType.MESH
F32 = jnp.float32
BF16 = jnp.bfloat16
NT = (((1,), (1,)), ((), ()))


def dot_nt(a, b):
    return lax.dot_general(a, b, NT, preferred_element_type=F32)


def dot_nn(a, b):
    return jnp.dot(a, b, preferred_element_type=F32)


def layer_kernel(
    q_ref, lk_ref, lv_ref, len_ref, res_ref, gain_ref,
    k_hbm, v_hbm, o_hbm, g_hbm, u_hbm, d_hbm,
    out_ref,
    kv, vv, ow, gw, uw, dw,
    qrow, lrow, csend, crecv, ag1, wide1, ag2, rsend, rrecv,
    resin, gainin, stream, gains, fsend, frecv,
    kvsem, wsem, wssem, wrsem, smallsem, smallrs,
    cssem, crsem, gssem, grsem, as1, ar1, as2, ar2, rss, rsr, fs, fr,
    ready,
):
    s = lax.axis_index("side")
    w = lax.axis_index("wide")
    x = lax.axis_index("narrow")
    z, y = w // 4, w % 4
    me = w * 4 + x
    other = (1 - s, w, x)

    def at(zz, yy, xx):
        return (s, zz * 4 + yy, xx)

    lines = [at(z, y, (x + k) % 4) for k in (1, 2, 3)]
    lines += [at(z, (y + k) % 4, x) for k in (1, 2, 3)]
    lines += [at((z + k) % 4, y, x) for k in (1, 2, 3)]

    def remote(src, dst, ssem, rsem, dev):
        return pltpu.make_async_remote_copy(
            src_ref=src, dst_ref=dst, send_sem=ssem, recv_sem=rsem,
            device_id=dev, device_id_type=MESH,
        )

    loads = []
    for i in range(2):
        for src, dst, j in ((k_hbm, kv, 0), (v_hbm, vv, 1)):
            c = pltpu.make_async_copy(src.at[i], dst.at[i], kvsem.at[2 * i + j])
            c.start()
            loads.append(c)
    barrier = pltpu.get_barrier_semaphore()
    for dev in lines + [other]:
        pl.semaphore_signal(barrier, inc=1, device_id=dev, device_id_type=MESH)
    weights = []
    for i, (src, dst, n) in enumerate(
        ((o_hbm, ow, 64), (g_hbm, gw, UNITS), (u_hbm, uw, UNITS), (d_hbm, dw, UNITS))
    ):
        dst = dst.at[pl.ds(s * 64, 64)] if i == 0 else dst.at[s]
        c = pltpu.make_async_copy(src, dst, wsem.at[i])
        c.start()
        weights.append((c, src, dst))

    qf = q_ref[...].astype(F32)
    for h in range(64):
        qrow[pl.ds(h, 2, stride=64), :] = qf[:, h * HEAD : (h + 1) * HEAD]
    for j, ref in enumerate((lk_ref, lv_ref)):
        lf = ref[...].astype(F32)
        for g in range(8):
            lrow[pl.ds(16 * j + g, 2, stride=8), :] = lf[:, g * HEAD : (g + 1) * HEAD]

    lane = lax.broadcasted_iota(jnp.int32, (1, HEAD), 1)
    low = lane < 64
    positions = x * SPAN + lax.broadcasted_iota(jnp.int32, (1, SPAN), 1)
    zero8 = jnp.zeros((8, HEAD), F32)

    def attend(i):
        valid = positions < len_ref[i]
        loads[2 * i].wait()
        for p in range(4):
            q16 = qrow[pl.ds(64 * i + 16 * p, 16), :]
            qa, qb = q16[:8], q16[8:]
            pair = jnp.concatenate(
                [jnp.concatenate([qa, zero8], 1), jnp.concatenate([zero8, qb], 1)], 0
            ).astype(BF16)
            lanes = slice(256 * p, 256 * (p + 1))
            score = dot_nt(pair, kv[i, :, lanes]) * SCALE
            score = jnp.where(valid, score, NEG)
            top = jnp.max(score, axis=1, keepdims=True)
            weight = jnp.where(valid, jnp.exp(score - top), 0.0)
            den = jnp.sum(weight, axis=1, keepdims=True)
            if p == 0:
                loads[2 * i + 1].wait()
            both = dot_nn(weight.astype(BF16), vv[i, :, lanes])
            num = jnp.concatenate([both[:8, :HEAD], both[8:, HEAD:]], 0)
            def rows(j):
                a = lrow[pl.ds(16 * j + 8 * i + 2 * p, 1), :]
                b = lrow[pl.ds(16 * j + 8 * i + 2 * p + 1, 1), :]
                return jnp.concatenate(
                    [jnp.broadcast_to(a, (8, HEAD)), jnp.broadcast_to(b, (8, HEAD))], 0
                )
            fresh = jnp.sum(q16 * rows(0), axis=1, keepdims=True) * SCALE
            fresh = jnp.where(x == 0, fresh, NEG)
            peak = jnp.maximum(top, fresh)
            shrink = jnp.exp(top - peak)
            own = jnp.where(x == 0, jnp.exp(fresh - peak), 0.0)
            num = num * shrink + own * rows(1)
            den = den * shrink + own
            m1 = peak.astype(BF16).astype(F32)
            m2 = (peak - m1).astype(BF16).astype(F32)
            m3 = (peak - m1) - m2
            d1 = den.astype(BF16).astype(F32)
            d2 = den - d1
            coded = jnp.where(
                lane == 0, m1,
                jnp.where(lane == 1, m2, jnp.where(lane == 2, m3, jnp.where(lane == 3, d1, d2))),
            )
            csend[p, pl.ds(16 * i, 16), :] = num.astype(BF16)
            csend[p, pl.ds(32 + 16 * i, 16), :] = coded.astype(BF16)

    attend(0)
    attend(1)

    pl.semaphore_wait(barrier, 10)
    combine = []
    for j, k in enumerate((2, 1, 3)):
        xx = (x + k) % 4
        c = remote(csend.at[xx], crecv.at[x], cssem, crsem, at(z, y, xx))
        c.start()
        combine.append(c)
    for dev in lines:
        pl.semaphore_signal(ready.at[0], inc=1, device_id=dev, device_id_type=MESH)

    small = [
        remote(res_ref.at[pl.ds((1 - s) * 32, 32)], resin, smallsem.at[0], smallrs.at[0], other),
        remote(gain_ref, gainin, smallsem.at[1], smallrs.at[1], other),
    ]
    for c in small:
        c.start()
    sends = []
    for i, (c, src, dst) in enumerate(weights):
        c = remote(src, dst, wssem.at[i], wrsem.at[i], other)
        c.start()
        sends.append(c)

    def halves(own, theirs):
        first = jnp.where(s == 0, own, theirs)
        second = jnp.where(s == 0, theirs, own)
        return jnp.concatenate([first, second], axis=1)

    for c in small:
        c.wait_recv()
    stream[...] = halves(
        res_ref[pl.ds(s * 32, 32), :].astype(F32), resin[...].astype(F32)
    )
    gains[me] = halves(gain_ref[...], gainin[...])

    def gain_stage(j, start, count, devs):
        part = gains.at[pl.ds(start, count)]
        cs = []
        for dev in devs:
            c = remote(part, part, gssem.at[j], grsem.at[j], dev)
            c.start()
            cs.append(c)
        return cs

    def settle(sem, ref, send=False):
        c = remote(ref, ref, sem, sem, other)
        if send:
            c.wait_send()
        else:
            c.wait_recv()

    gain_stage(0, me, 1, lines[:3])
    pl.semaphore_wait(ready.at[0], 9)
    for dev in lines:
        pl.semaphore_signal(ready.at[1], inc=1, device_id=dev, device_id_type=MESH)

    settle(crsem, crecv.at[pl.ds(0, 3)])
    crecv[x] = csend[x]
    parts = []
    for i in range(4):
        code = crecv[i, 32:64, :].astype(F32)
        m = code[:, 0:1] + code[:, 1:2] + code[:, 2:3]
        d = code[:, 3:4] + code[:, 4:5]
        parts.append((m, d, crecv[i, 0:32, :].astype(F32)))
    peak = jnp.maximum(
        jnp.maximum(parts[0][0], parts[1][0]), jnp.maximum(parts[2][0], parts[3][0])
    )
    num, den = 0.0, 0.0
    for m, d, n in parts:
        f = jnp.exp(m - peak)
        num = num + n * f
        den = den + d * f
    ag1[me] = (num / den).astype(BF16)

    pl.semaphore_wait(ready.at[1], 9)

    order = (2, 1, 3, 0)

    def spread(buf, ssem, rsem, by):
        for g in order:
            def step(i, carry, g=g):
                a, b = i // 4, i % 4
                if by == "x":
                    dev = at((z + a) % 4, (y + b) % 4, (x + g) % 4)
                else:
                    dev = at((z + g) % 4, (y + a) % 4, (x + b) % 4)
                remote(buf.at[me], buf.at[me], ssem, rsem.at[g], dev).start()
                return carry
            lax.fori_loop(1 if g == 0 else 0, 16, step, 0)

    spread(ag1, as1, ar1, "x")

    settle(grsem.at[0], gains.at[pl.ds(0, 3)])
    gain_stage(1, w * 4, 4, lines[3:6])

    weights[0][0].wait()
    sends[0].wait_recv()
    total = stream[...]
    for g in order:
        settle(ar1.at[g], ag1.at[pl.ds(0, 15 if g == 0 else 16)])
        xx = (x + 4 - g) % 4
        for n in range(16):
            wide1[g, pl.ds(32 * n, 32), :] = ag1[4 * n + xx].astype(F32)
        rows = jnp.concatenate(
            [wide1[g, pl.ds(h, 32, stride=16), :].astype(BF16) for h in range(16)], axis=1
        )
        total = total + dot_nt(rows, ow[:, pl.ds(pl.multiple_of(xx * 2048, 2048), 2048)])
    rounded = total.astype(BF16)
    stream[...] = rounded.astype(F32)
    ag2[me] = rounded

    spread(ag2, as2, ar2, "z")

    settle(grsem.at[1], gains.at[pl.ds(0, 12)])
    gain_stage(2, z * 16, 16, lines[6:9])
    for c, _, _ in weights[1:3]:
        c.wait()
    for c in sends[1:3]:
        c.wait_recv()
    settle(grsem.at[2], gains.at[pl.ds(0, 48)])

    squares = jnp.zeros((32, HEAD), F32)
    gate = [jnp.zeros((32, UNITS), F32) for _ in range(2)]
    up = [jnp.zeros((32, UNITS), F32) for _ in range(2)]
    for g in order:
        settle(ar2.at[g], ag2.at[pl.ds(0, 15 if g == 0 else 16)])
        zz = (z + 4 - g) % 4
        firsts, seconds = [], []
        for t in range(8):
            c = zz * 16 + 2 * t
            a, b = ag2[c].astype(F32), ag2[c + 1].astype(F32)
            squares = squares + a * a + b * b
            a = a * gains[c][0:1]
            b = b * gains[c + 1][0:1]
            firsts.append(jnp.where(low, a, pltpu.roll(b, 64, 1)).astype(BF16))
            seconds.append(jnp.where(low, pltpu.roll(a, 64, 1), b).astype(BF16))
        first = jnp.concatenate(firsts, axis=1)
        second = jnp.concatenate(seconds, axis=1)
        at0 = pl.ds(pl.multiple_of(zz * 1024, 1024), 1024)
        at1 = pl.ds(pl.multiple_of(4096 + zz * 1024, 1024), 1024)
        for e in range(2):
            gate[e] = gate[e] + dot_nt(first, gw[e, :, at0]) + dot_nt(second, gw[e, :, at1])
            up[e] = up[e] + dot_nt(first, uw[e, :, at0]) + dot_nt(second, uw[e, :, at1])
    inverse = lax.rsqrt(jnp.sum(squares, axis=1, keepdims=True) / D + 1e-05)
    hidden = []
    for e in range(2):
        v = gate[e] * inverse
        hidden.append((v / (1.0 + jnp.exp(-v)) * (up[e] * inverse)).astype(BF16))

    weights[3][0].wait()
    sends[3].wait_recv()
    for g in order:
        zz = (z + g) % 4
        at0 = pl.ds(pl.multiple_of(zz * 1024, 1024), 1024)
        at1 = pl.ds(pl.multiple_of(4096 + zz * 1024, 1024), 1024)
        first = dot_nn(hidden[0], dw[0, :, at0]) + dot_nn(hidden[1], dw[1, :, at0])
        second = dot_nn(hidden[0], dw[0, :, at1]) + dot_nn(hidden[1], dw[1, :, at1])
        for t in range(8):
            a = first[:, HEAD * t : HEAD * (t + 1)]
            b = second[:, HEAD * t : HEAD * (t + 1)]
            rsend[zz * 16 + 2 * t] = jnp.where(low, a, pltpu.roll(b, 64, 1)).astype(BF16)
            rsend[zz * 16 + 2 * t + 1] = jnp.where(low, pltpu.roll(a, 64, 1), b).astype(BF16)

        def step(i, carry, zz=zz, g=g):
            yy, xx = (y + i // 4) % 4, (x + i % 4) % 4
            remote(
                rsend.at[zz * 16 + yy * 4 + xx], rrecv.at[me], rss, rsr.at[g], at(zz, yy, xx)
            ).start()
            return carry

        lax.fori_loop(1 if g == 0 else 0, 16, step, 0)
    rrecv[me] = rsend[me]

    total = stream[...]
    for g in order:
        settle(rsr.at[g], rrecv.at[pl.ds(0, 15 if g == 0 else 16)])
        zz = (z + 4 - g) % 4
        part = rrecv[zz * 16].astype(F32)
        for n in range(1, 16):
            part = part + rrecv[zz * 16 + n].astype(F32)
        total = total + part
    turned = pltpu.roll(total, 64, 1)
    mine = jnp.where(s == 0, total, turned)[:, :64].astype(BF16)
    theirs = jnp.where(s == 0, turned, total)[:, :64].astype(BF16)
    fsend[...] = theirs
    last = remote(fsend, frecv, fs, fr, other)
    last.start()
    out_ref[pl.ds(s * 32, 32), :] = mine

    settle(cssem, csend.at[pl.ds(0, 3)], True)
    for c in small + sends:
        c.wait_send()
    settle(gssem.at[0], gains.at[pl.ds(0, 3)], True)
    settle(gssem.at[1], gains.at[pl.ds(0, 12)], True)
    settle(gssem.at[2], gains.at[pl.ds(0, 48)], True)
    settle(as1, ag1.at[pl.ds(0, 63)], True)
    settle(as2, ag2.at[pl.ds(0, 63)], True)
    settle(rss, rsend.at[pl.ds(0, 63)], True)
    last.wait()
    out_ref[pl.ds((1 - s) * 32, 32), :] = frecv[...]


def on_device(
    queries, key_cache, value_cache, latest_key, latest_value, lengths,
    residual, o_weight, norm_gain, gate_weight, up_weight, down_weight,
):
    gain = jnp.broadcast_to(norm_gain.astype(F32)[None, :], (8, 64))
    vmem = pl.BlockSpec(memory_space=pltpu.VMEM)
    smem = pl.BlockSpec(memory_space=pltpu.SMEM)
    hbm = pl.BlockSpec(memory_space=pl.ANY)
    dma = pltpu.SemaphoreType.DMA
    return pl.pallas_call(
        layer_kernel,
        out_shape=jax.ShapeDtypeStruct((64, 64), BF16),
        in_specs=[vmem, vmem, vmem, smem, vmem, vmem] + [hbm] * 6,
        out_specs=vmem,
        scratch_shapes=[
            pltpu.VMEM((2, SPAN, 1024), BF16),
            pltpu.VMEM((2, SPAN, 1024), BF16),
            pltpu.VMEM((128, D), BF16),
            pltpu.VMEM((2, UNITS, D), BF16),
            pltpu.VMEM((2, UNITS, D), BF16),
            pltpu.VMEM((2, UNITS, D), BF16),
            pltpu.VMEM((128, HEAD), F32),
            pltpu.VMEM((32, HEAD), F32),
            pltpu.VMEM((4, 64, HEAD), BF16),
            pltpu.VMEM((4, 64, HEAD), BF16),
            pltpu.VMEM((64, 32, HEAD), BF16),
            pltpu.VMEM((4, 512, HEAD), F32),
            pltpu.VMEM((64, 32, HEAD), BF16),
            pltpu.VMEM((64, 32, HEAD), BF16),
            pltpu.VMEM((64, 32, HEAD), BF16),
            pltpu.VMEM((32, 64), BF16),
            pltpu.VMEM((8, 64), F32),
            pltpu.VMEM((32, HEAD), F32),
            pltpu.VMEM((64, 8, HEAD), F32),
            pltpu.VMEM((32, 64), BF16),
            pltpu.VMEM((32, 64), BF16),
            dma((4,)), dma((4,)), dma((4,)), dma((4,)), dma((2,)), dma((2,)),
            dma, dma, dma((3,)), dma((3,)),
            dma, dma((4,)), dma, dma((4,)), dma, dma((4,)), dma, dma,
            pltpu.SemaphoreType.REGULAR((2,)),
        ],
        compiler_params=pltpu.CompilerParams(
            collective_id=0, has_side_effects=True, vmem_limit_bytes=52 << 20
        ),
    )(
        queries, latest_key, latest_value, lengths, residual, gain,
        key_cache, value_cache, o_weight.T, gate_weight.T, up_weight.T, down_weight,
    )


def solution(mesh):
    sessions = ("side", "wide")
    every = ("side", "wide", "narrow")
    return jax.shard_map(
        on_device,
        mesh=mesh,
        in_specs=(
            P(sessions, None),
            P(sessions, "narrow", None),
            P(sessions, "narrow", None),
            P(sessions, None),
            P(sessions, None),
            P(sessions),
            P(None, every),
            P(None, every),
            P(every),
            P(None, every),
            P(None, every),
            P(every, None),
        ),
        out_specs=P(None, every),
        check_vma=False,
    )
```

```python
import jax
import jax.numpy as jnp
from jax import lax
from jax.experimental import pallas as pl
from jax.experimental.pallas import tpu as pltpu
from jax.sharding import PartitionSpec as P

D = 8192
HEAD = 128
SPAN = 1024
UNITS = 224
SCALE = HEAD**-0.5
NEG = -1e30
MESH = pl.DeviceIdType.MESH
F32 = jnp.float32
BF16 = jnp.bfloat16
NT = (((1,), (1,)), ((), ()))


def dot_nt(a, b):
    return lax.dot_general(a, b, NT, preferred_element_type=F32)


def dot_nn(a, b):
    return jnp.dot(a, b, preferred_element_type=F32)


def layer_kernel(
    q_hbm, lk_hbm, lv_hbm, len_hbm, res_hbm, gain_hbm,
    k_hbm, v_hbm, o_hbm, g_hbm, u_hbm, d_hbm,
    out_ref,
    q_ref, lk_ref, lv_ref, len_ref, res_ref, gain1, gain_ref, insem,
    kv, vv, ow, gw, uw, dw,
    qrow, lrow, csend, crecv, ag1, perm, ag2, gnat, rsend, rrecv,
    resin, gainin, stream, gains, fsend, frecv,
    kvsem, wsem, wssem, wrsem, smallsem, smallrs,
    cssem, crsem, gssem, grsem, as1, ar1, as2, ar2, rss, rsr, fs, fr,
    ready,
):
    s = lax.axis_index("side")
    w = lax.axis_index("wide")
    x = lax.axis_index("narrow")
    z, y = w // 4, w % 4
    me = w * 4 + x
    other = (1 - s, w, x)

    def at(zz, yy, xx):
        return (s, zz * 4 + yy, xx)

    lines = [at(z, y, (x + k) % 4) for k in (1, 2, 3)]
    lines += [at(z, (y + k) % 4, x) for k in (1, 2, 3)]
    lines += [at((z + k) % 4, y, x) for k in (1, 2, 3)]

    def remote(src, dst, ssem, rsem, dev):
        return pltpu.make_async_remote_copy(
            src_ref=src, dst_ref=dst, send_sem=ssem, recv_sem=rsem,
            device_id=dev, device_id_type=MESH,
        )

    inputs = []
    for i, (src, dst) in enumerate(
        (
            (q_hbm, q_ref), (lk_hbm, lk_ref), (lv_hbm, lv_ref),
            (len_hbm, len_ref), (res_hbm, res_ref), (gain_hbm, gain1),
        )
    ):
        c = pltpu.make_async_copy(src, dst, insem.at[i])
        c.start()
        inputs.append(c)
    loads = []
    for i in range(2):
        for src, dst, j in ((k_hbm, kv, 0), (v_hbm, vv, 1)):
            c = pltpu.make_async_copy(src.at[i], dst.at[i], kvsem.at[2 * i + j])
            c.start()
            loads.append(c)
    barrier = pltpu.get_barrier_semaphore()
    for dev in lines + [other]:
        pl.semaphore_signal(barrier, inc=1, device_id=dev, device_id_type=MESH)
    for c in inputs:
        c.wait()
    gain_ref[...] = jnp.broadcast_to(gain1[...].astype(F32)[None, :], (8, 64))

    qf = q_ref[...].astype(F32)
    for h in range(64):
        qrow[pl.ds(h, 2, stride=64), :] = qf[:, h * HEAD : (h + 1) * HEAD]
    for j, ref in enumerate((lk_ref, lv_ref)):
        lf = ref[...].astype(F32)
        for g in range(8):
            lrow[pl.ds(16 * j + g, 2, stride=8), :] = lf[:, g * HEAD : (g + 1) * HEAD]

    lane = lax.broadcasted_iota(jnp.int32, (1, HEAD), 1)
    low = lane < 64
    positions = x * SPAN + lax.broadcasted_iota(jnp.int32, (1, SPAN), 1)
    zero8 = jnp.zeros((8, HEAD), F32)

    weights = []

    def fetch():
        for i, (src, dst, n) in enumerate(
            ((o_hbm, ow, 64), (g_hbm, gw, UNITS), (u_hbm, uw, UNITS), (d_hbm, dw, UNITS))
        ):
            dst = dst.at[pl.ds(s * n, n)]
            c = pltpu.make_async_copy(src, dst, wsem.at[i])
            c.start()
            weights.append((c, src, dst))

    def attend(i):
        valid = positions < len_ref[i]
        queries = [qrow[pl.ds(64 * i + 16 * p, 16), :] for p in range(4)]
        pairs = []
        for q16 in queries:
            pairs.append(
                jnp.concatenate(
                    [
                        jnp.concatenate([q16[:8], zero8], 1),
                        jnp.concatenate([zero8, q16[8:]], 1),
                    ],
                    0,
                ).astype(BF16)
            )

        def repeated(j):
            return jnp.concatenate(
                [
                    jnp.broadcast_to(lrow[pl.ds(16 * j + 8 * i + g, 1), :], (8, HEAD))
                    for g in range(8)
                ],
                0,
            )

        fresh = jnp.sum(jnp.concatenate(queries, 0) * repeated(0), axis=1, keepdims=True) * SCALE
        fresh = jnp.where(x == 0, fresh, NEG)
        loads[2 * i].wait()
        score = jnp.concatenate(
            [dot_nt(pairs[p], kv[i, :, 256 * p : 256 * (p + 1)]) for p in range(4)], 0
        )
        score = jnp.where(valid, score * SCALE, NEG)
        top = jnp.max(score, axis=1, keepdims=True)
        weight = jnp.where(valid, jnp.exp(score - top), 0.0)
        den = jnp.sum(weight, axis=1, keepdims=True)
        rounded = weight.astype(BF16)
        loads[2 * i + 1].wait()
        nums = []
        for p in range(4):
            both = dot_nn(rounded[16 * p : 16 * p + 16], vv[i, :, 256 * p : 256 * (p + 1)])
            nums += [both[:8, :HEAD], both[8:, HEAD:]]
        num = jnp.concatenate(nums, 0)
        peak = jnp.maximum(top, fresh)
        shrink = jnp.exp(top - peak)
        own = jnp.where(x == 0, jnp.exp(fresh - peak), 0.0)
        num = num * shrink + own * repeated(1)
        den = den * shrink + own
        m1 = peak.astype(BF16).astype(F32)
        m2 = (peak - m1).astype(BF16).astype(F32)
        m3 = (peak - m1) - m2
        d1 = den.astype(BF16).astype(F32)
        d2 = den - d1
        coded = jnp.where(
            lane == 0, m1,
            jnp.where(lane == 1, m2, jnp.where(lane == 2, m3, jnp.where(lane == 3, d1, d2))),
        )
        num, coded = num.astype(BF16), coded.astype(BF16)
        for p in range(4):
            csend[p, pl.ds(16 * i, 16), :] = num[16 * p : 16 * p + 16]
            csend[p, pl.ds(32 + 16 * i, 16), :] = coded[16 * p : 16 * p + 16]

    attend(0)
    fetch()
    attend(1)

    r = lax.broadcasted_iota(jnp.int32, (256, 256), 0)
    k = lax.broadcasted_iota(jnp.int32, (256, 256), 1)
    source = (r % 16 // 2) * 32 + (r % 2) * 16 + r // 16
    perm[...] = jnp.where(source == k, 1.0, 0.0).astype(BF16)

    pl.semaphore_wait(barrier, 10)
    combine = []
    for j, k in enumerate((2, 1, 3)):
        xx = (x + k) % 4
        c = remote(csend.at[xx], crecv.at[x], cssem, crsem, at(z, y, xx))
        c.start()
        combine.append(c)
    for dev in lines:
        pl.semaphore_signal(ready.at[0], inc=1, device_id=dev, device_id_type=MESH)

    small = [
        remote(res_ref.at[pl.ds((1 - s) * 32, 32)], resin, smallsem.at[0], smallrs.at[0], other),
        remote(gain_ref, gainin, smallsem.at[1], smallrs.at[1], other),
    ]
    for c in small:
        c.start()
    sends = []
    for i, (c, src, dst) in enumerate(weights):
        c = remote(src, dst, wssem.at[i], wrsem.at[i], other)
        c.start()
        sends.append(c)

    def halves(own, theirs):
        first = jnp.where(s == 0, own, theirs)
        second = jnp.where(s == 0, theirs, own)
        return jnp.concatenate([first, second], axis=1)

    for c in small:
        c.wait_recv()
    stream[...] = halves(
        res_ref[pl.ds(s * 32, 32), :].astype(F32), resin[...].astype(F32)
    )
    gains[me] = halves(gain_ref[...], gainin[...])

    def gain_stage(j, start, count, devs):
        part = gains.at[pl.ds(start, count)]
        cs = []
        for dev in devs:
            c = remote(part, part, gssem.at[j], grsem.at[j], dev)
            c.start()
            cs.append(c)
        return cs

    def settle(sem, ref, send=False):
        c = remote(ref, ref, sem, sem, other)
        if send:
            c.wait_send()
        else:
            c.wait_recv()

    gain_stage(0, me, 1, lines[:3])
    pl.semaphore_wait(ready.at[0], 9)
    for dev in lines:
        pl.semaphore_signal(ready.at[1], inc=1, device_id=dev, device_id_type=MESH)

    settle(crsem, crecv.at[pl.ds(0, 3)])
    crecv[x] = csend[x]
    parts = []
    for i in range(4):
        code = crecv[i, 32:64, :].astype(F32)
        m = code[:, 0:1] + code[:, 1:2] + code[:, 2:3]
        d = code[:, 3:4] + code[:, 4:5]
        parts.append((m, d, crecv[i, 0:32, :].astype(F32)))
    peak = jnp.maximum(
        jnp.maximum(parts[0][0], parts[1][0]), jnp.maximum(parts[2][0], parts[3][0])
    )
    num, den = 0.0, 0.0
    for m, d, n in parts:
        f = jnp.exp(m - peak)
        num = num + n * f
        den = den + d * f
    ag1[me] = (num / den).astype(BF16)

    pl.semaphore_wait(ready.at[1], 9)

    order = (2, 1, 3, 0)
    arrival = (0, 1, 3, 2)

    def each(g, step):
        if g == 0:
            lax.fori_loop(0, 10, step, 0)
            lax.fori_loop(11, 16, step, 0)
        else:
            lax.fori_loop(0, 16, step, 0)

    def spread(buf, ssem, rsem, by):
        for g in order:
            def step(i, carry, g=g):
                a, b = (i // 4 + 2) % 4, (i + 2) % 4
                if by == "x":
                    dev = at((z + a) % 4, (y + b) % 4, (x + g) % 4)
                else:
                    dev = at((z + g) % 4, (y + a) % 4, (x + b) % 4)
                remote(buf.at[me], buf.at[me], ssem, rsem.at[g], dev).start()
                return carry
            each(g, step)

    spread(ag1, as1, ar1, "x")

    settle(grsem.at[0], gains.at[pl.ds(0, 3)])
    gain_stage(1, w * 4, 4, lines[3:6])

    weights[0][0].wait()
    sends[0].wait_recv()
    total = stream[...]
    for n, g in enumerate(arrival):
        settle(ar1.at[g], ag1.at[pl.ds(0, 15 if g == 0 else 16)])
        xx = (x + 4 - g) % 4
        turned = []
        for half in range(2):
            rows = jnp.concatenate([ag1[4 * (8 * half + j) + xx] for j in range(8)], 0)
            turned.append(dot_nn(perm[...], rows).astype(BF16))
        rows = jnp.concatenate(
            [
                jnp.concatenate([part[16 * h : 16 * h + 16] for part in turned], 0)
                for h in range(16)
            ],
            axis=1,
        )
        total = total + dot_nt(rows, ow[:, pl.ds(pl.multiple_of(xx * 2048, 2048), 2048)])
        if n == 1:
            settle(grsem.at[1], gains.at[pl.ds(0, 12)])
            gain_stage(2, z * 16, 16, lines[6:9])
    rounded = total.astype(BF16)
    stream[...] = rounded.astype(F32)
    ag2[me] = rounded

    spread(ag2, as2, ar2, "z")

    def mixed(a, b):
        m = pltpu.roll(jnp.where(low, b, a), 64, 1)
        return jnp.where(low, a, m), jnp.where(low, m, b)

    settle(grsem.at[2], gains.at[pl.ds(0, 48)])
    for t in range(32):
        first, second = mixed(gains[2 * t], gains[2 * t + 1])
        gnat[:, HEAD * t : HEAD * (t + 1)] = jnp.concatenate([first, first], 0).astype(BF16)
        gnat[:, 4096 + HEAD * t : 4096 + HEAD * (t + 1)] = jnp.concatenate(
            [second, second], 0
        ).astype(BF16)
    for c, _, _ in weights[1:3]:
        c.wait()
    for c in sends[1:3]:
        c.wait_recv()

    squares = jnp.zeros((32, 32), F32)
    gate = jnp.zeros((32, 2 * UNITS), F32)
    up = jnp.zeros((32, 2 * UNITS), F32)
    for g in arrival:
        settle(ar2.at[g], ag2.at[pl.ds(0, 15 if g == 0 else 16)])
        zz = (z + 4 - g) % 4
        sides = [[], []]
        for t in range(8):
            c = zz * 16 + 2 * t
            for e, part in enumerate(mixed(ag2[c].astype(F32), ag2[c + 1].astype(F32))):
                sides[e].append(part.astype(BF16))
        for e in range(2):
            part = jnp.concatenate(sides[e], axis=1)
            squares = squares + dot_nt(part, part)
            lanes = pl.ds(pl.multiple_of(4096 * e + zz * 1024, 1024), 1024)
            row = gnat[:, lanes]
            part = part * jnp.concatenate([row, row], 0)
            gate = gate + dot_nt(part, gw[:, lanes])
            up = up + dot_nt(part, uw[:, lanes])
    diagonal = lax.broadcasted_iota(jnp.int32, (32, 32), 0) == lax.broadcasted_iota(
        jnp.int32, (32, 32), 1
    )
    squares = jnp.sum(jnp.where(diagonal, squares, 0.0), axis=1, keepdims=True)
    inverse = lax.rsqrt(squares / D + 1e-05)
    v = gate * inverse
    hidden = (v / (1.0 + jnp.exp(-v)) * (up * inverse)).astype(BF16)

    weights[3][0].wait()
    sends[3].wait_recv()
    for g in order:
        zz = (z + g) % 4
        at0 = pl.ds(pl.multiple_of(zz * 1024, 1024), 1024)
        at1 = pl.ds(pl.multiple_of(4096 + zz * 1024, 1024), 1024)
        first = dot_nn(hidden, dw[:, at0])
        second = dot_nn(hidden, dw[:, at1])
        for t in range(8):
            lanes = slice(HEAD * t, HEAD * (t + 1))
            a, b = mixed(first[:, lanes], second[:, lanes])
            rsend[zz * 16 + 2 * t] = a.astype(BF16)
            rsend[zz * 16 + 2 * t + 1] = b.astype(BF16)

        def step(i, carry, zz=zz, g=g):
            yy, xx = (y + i // 4 + 2) % 4, (x + i + 2) % 4
            remote(
                rsend.at[zz * 16 + yy * 4 + xx], rrecv.at[me], rss, rsr.at[g], at(zz, yy, xx)
            ).start()
            return carry

        each(g, step)
    rrecv[me] = rsend[me]

    total = stream[...]
    for g in arrival:
        settle(rsr.at[g], rrecv.at[pl.ds(0, 15 if g == 0 else 16)])
        zz = (z + 4 - g) % 4
        part = rrecv[zz * 16].astype(F32)
        for n in range(1, 16):
            part = part + rrecv[zz * 16 + n].astype(F32)
        total = total + part
    turned = pltpu.roll(total, 64, 1)
    mine = jnp.where(s == 0, total, turned)[:, :64].astype(BF16)
    theirs = jnp.where(s == 0, turned, total)[:, :64].astype(BF16)
    fsend[...] = theirs
    last = remote(fsend, frecv, fs, fr, other)
    last.start()
    out_ref[pl.ds(s * 32, 32), :] = mine

    settle(cssem, csend.at[pl.ds(0, 3)], True)
    for c in small + sends:
        c.wait_send()
    settle(gssem.at[0], gains.at[pl.ds(0, 3)], True)
    settle(gssem.at[1], gains.at[pl.ds(0, 12)], True)
    settle(gssem.at[2], gains.at[pl.ds(0, 48)], True)
    settle(as1, ag1.at[pl.ds(0, 63)], True)
    settle(as2, ag2.at[pl.ds(0, 63)], True)
    settle(rss, rsend.at[pl.ds(0, 63)], True)
    last.wait()
    out_ref[pl.ds((1 - s) * 32, 32), :] = frecv[...]


def on_device(
    queries, key_cache, value_cache, latest_key, latest_value, lengths,
    residual, o_weight, norm_gain, gate_weight, up_weight, down_weight,
):
    vmem = pl.BlockSpec(memory_space=pltpu.VMEM)
    hbm = pl.BlockSpec(memory_space=pltpu.HBM)
    dma = pltpu.SemaphoreType.DMA
    return pl.pallas_call(
        layer_kernel,
        out_shape=jax.ShapeDtypeStruct((64, 64), BF16),
        in_specs=[hbm] * 12,
        out_specs=vmem,
        scratch_shapes=[
            pltpu.VMEM((2, D), BF16),
            pltpu.VMEM((2, 1024), BF16),
            pltpu.VMEM((2, 1024), BF16),
            pltpu.SMEM((2,), jnp.int32),
            pltpu.VMEM((64, 64), BF16),
            pltpu.VMEM((64,), BF16),
            pltpu.VMEM((8, 64), F32),
            dma((6,)),
            pltpu.VMEM((2, SPAN, 1024), BF16),
            pltpu.VMEM((2, SPAN, 1024), BF16),
            pltpu.VMEM((128, D), BF16),
            pltpu.VMEM((2 * UNITS, D), BF16),
            pltpu.VMEM((2 * UNITS, D), BF16),
            pltpu.VMEM((2 * UNITS, D), BF16),
            pltpu.VMEM((128, HEAD), F32),
            pltpu.VMEM((32, HEAD), F32),
            pltpu.VMEM((4, 64, HEAD), BF16),
            pltpu.VMEM((4, 64, HEAD), BF16),
            pltpu.VMEM((64, 32, HEAD), BF16),
            pltpu.VMEM((256, 256), BF16),
            pltpu.VMEM((64, 32, HEAD), BF16),
            pltpu.VMEM((16, D), BF16),
            pltpu.VMEM((64, 32, HEAD), BF16),
            pltpu.VMEM((64, 32, HEAD), BF16),
            pltpu.VMEM((32, 64), BF16),
            pltpu.VMEM((8, 64), F32),
            pltpu.VMEM((32, HEAD), F32),
            pltpu.VMEM((64, 8, HEAD), F32),
            pltpu.VMEM((32, 64), BF16),
            pltpu.VMEM((32, 64), BF16),
            dma((4,)), dma((4,)), dma((4,)), dma((4,)), dma((2,)), dma((2,)),
            dma, dma, dma((3,)), dma((3,)),
            dma, dma((4,)), dma, dma((4,)), dma, dma((4,)), dma, dma,
            pltpu.SemaphoreType.REGULAR((2,)),
        ],
        compiler_params=pltpu.CompilerParams(
            collective_id=0, has_side_effects=True, vmem_limit_bytes=64 << 20
        ),
    )(
        queries, latest_key, latest_value, lengths, residual, norm_gain,
        key_cache, value_cache, o_weight.T, gate_weight.T, up_weight.T, down_weight,
    )


def solution(mesh):
    sessions = ("side", "wide")
    every = ("side", "wide", "narrow")
    return jax.shard_map(
        on_device,
        mesh=mesh,
        in_specs=(
            P(sessions, None),
            P(sessions, "narrow", None),
            P(sessions, "narrow", None),
            P(sessions, None),
            P(sessions, None),
            P(sessions),
            P(None, every),
            P(None, every),
            P(every),
            P(None, every),
            P(None, every),
            P(every, None),
        ),
        out_specs=P(None, every),
        check_vma=False,
    )
```

```python
import jax
import jax.numpy as jnp
from jax import lax
from jax.experimental import pallas as pl
from jax.experimental.pallas import tpu as pltpu
from jax.sharding import PartitionSpec as P

D = 8192
HEAD = 128
SPAN = 1024
UNITS = 224
SCALE = HEAD**-0.5
NEG = -1e30
MESH = pl.DeviceIdType.MESH
F32 = jnp.float32
BF16 = jnp.bfloat16
NT = (((1,), (1,)), ((), ()))


def dot_nt(a, b):
    return lax.dot_general(a, b, NT, preferred_element_type=F32)


def dot_nn(a, b):
    return jnp.dot(a, b, preferred_element_type=F32)


def layer_kernel(
    q_hbm, lk_hbm, lv_hbm, len_hbm, res_hbm, gain_hbm,
    k_hbm, v_hbm, o_hbm, g_hbm, u_hbm, d_hbm,
    out_ref,
    q_ref, lk_ref, lv_ref, len_ref, res_ref, gain1, gain_ref, insem,
    kv, vv, ow, gw, uw, dw,
    qrow, lrow, csend, crecv, ag1, perm, ag2, gnat, rsend, rrecv,
    resin, gainin, stream, gains, fsend, frecv,
    kvsem, wsem, wssem, wrsem, smallsem, smallrs,
    cssem, crsem, gssem, grsem, as1, ar1, as2, ar2, rss, rsr, fs, fr,
    ready,
):
    s = lax.axis_index("side")
    w = lax.axis_index("wide")
    x = lax.axis_index("narrow")
    z, y = w // 4, w % 4
    me = w * 4 + x
    other = (1 - s, w, x)

    def at(zz, yy, xx):
        return (s, zz * 4 + yy, xx)

    lines = [at(z, y, (x + k) % 4) for k in (1, 2, 3)]
    lines += [at(z, (y + k) % 4, x) for k in (1, 2, 3)]
    lines += [at((z + k) % 4, y, x) for k in (1, 2, 3)]

    def remote(src, dst, ssem, rsem, dev):
        return pltpu.make_async_remote_copy(
            src_ref=src, dst_ref=dst, send_sem=ssem, recv_sem=rsem,
            device_id=dev, device_id_type=MESH,
        )

    inputs = []
    for i, (src, dst) in enumerate(
        (
            (q_hbm, q_ref), (lk_hbm, lk_ref), (lv_hbm, lv_ref),
            (len_hbm, len_ref), (res_hbm, res_ref), (gain_hbm, gain1),
        )
    ):
        c = pltpu.make_async_copy(src, dst, insem.at[i])
        c.start()
        inputs.append(c)
    loads = []
    for i in range(2):
        for src, dst, j in ((k_hbm, kv, 0), (v_hbm, vv, 1)):
            c = pltpu.make_async_copy(src.at[i], dst.at[i], kvsem.at[2 * i + j])
            c.start()
            loads.append(c)
    barrier = pltpu.get_barrier_semaphore()
    for dev in lines + [other]:
        pl.semaphore_signal(barrier, inc=1, device_id=dev, device_id_type=MESH)
    for c in inputs:
        c.wait()
    gain_ref[...] = jnp.broadcast_to(gain1[...].astype(F32)[None, :], (8, 64))

    qf = q_ref[...].astype(F32)
    for h in range(64):
        qrow[pl.ds(h, 2, stride=64), :] = qf[:, h * HEAD : (h + 1) * HEAD]
    for j, ref in enumerate((lk_ref, lv_ref)):
        lf = ref[...].astype(F32)
        for g in range(8):
            lrow[pl.ds(16 * j + g, 2, stride=8), :] = lf[:, g * HEAD : (g + 1) * HEAD]

    lane = lax.broadcasted_iota(jnp.int32, (1, HEAD), 1)
    low = lane < 64
    positions = x * SPAN + lax.broadcasted_iota(jnp.int32, (1, SPAN), 1)
    zero8 = jnp.zeros((8, HEAD), F32)

    weights = []

    def fetch():
        for i, (src, dst, n) in enumerate(
            ((o_hbm, ow, 64), (g_hbm, gw, UNITS), (u_hbm, uw, UNITS), (d_hbm, dw, UNITS))
        ):
            dst = dst.at[pl.ds(s * n, n)]
            c = pltpu.make_async_copy(src, dst, wsem.at[i])
            c.start()
            weights.append((c, src, dst))

    def attend(i):
        valid = positions < len_ref[i]
        queries = [qrow[pl.ds(64 * i + 16 * p, 16), :] for p in range(4)]
        pairs = []
        for q16 in queries:
            pairs.append(
                jnp.concatenate(
                    [
                        jnp.concatenate([q16[:8], zero8], 1),
                        jnp.concatenate([zero8, q16[8:]], 1),
                    ],
                    0,
                ).astype(BF16)
            )

        def repeated(j):
            return jnp.concatenate(
                [
                    jnp.broadcast_to(lrow[pl.ds(16 * j + 8 * i + g, 1), :], (8, HEAD))
                    for g in range(8)
                ],
                0,
            )

        fresh = jnp.sum(jnp.concatenate(queries, 0) * repeated(0), axis=1, keepdims=True) * SCALE
        fresh = jnp.where(x == 0, fresh, NEG)
        loads[2 * i].wait()
        score = jnp.concatenate(
            [dot_nt(pairs[p], kv[i, :, 256 * p : 256 * (p + 1)]) for p in range(4)], 0
        )
        score = jnp.where(valid, score * SCALE, NEG)
        top = jnp.max(score, axis=1, keepdims=True)
        weight = jnp.where(valid, jnp.exp(score - top), 0.0)
        den = jnp.sum(weight, axis=1, keepdims=True)
        rounded = weight.astype(BF16)
        loads[2 * i + 1].wait()
        nums = []
        for p in range(4):
            both = dot_nn(rounded[16 * p : 16 * p + 16], vv[i, :, 256 * p : 256 * (p + 1)])
            nums += [both[:8, :HEAD], both[8:, HEAD:]]
        num = jnp.concatenate(nums, 0)
        peak = jnp.maximum(top, fresh)
        shrink = jnp.exp(top - peak)
        own = jnp.where(x == 0, jnp.exp(fresh - peak), 0.0)
        num = num * shrink + own * repeated(1)
        den = den * shrink + own
        m1 = peak.astype(BF16).astype(F32)
        m2 = (peak - m1).astype(BF16).astype(F32)
        m3 = (peak - m1) - m2
        d1 = den.astype(BF16).astype(F32)
        d2 = den - d1
        coded = jnp.where(
            lane == 0, m1,
            jnp.where(lane == 1, m2, jnp.where(lane == 2, m3, jnp.where(lane == 3, d1, d2))),
        )
        num, coded = num.astype(BF16), coded.astype(BF16)
        for p in range(4):
            csend[p, pl.ds(16 * i, 16), :] = num[16 * p : 16 * p + 16]
            csend[p, pl.ds(32 + 16 * i, 16), :] = coded[16 * p : 16 * p + 16]

    attend(0)
    fetch()
    attend(1)

    r = lax.broadcasted_iota(jnp.int32, (256, 256), 0)
    k = lax.broadcasted_iota(jnp.int32, (256, 256), 1)
    source = (r % 16 // 2) * 32 + (r % 2) * 16 + r // 16
    perm[...] = jnp.where(source == k, 1.0, 0.0).astype(BF16)

    pl.semaphore_wait(barrier, 10)
    combine = []
    for j, k in enumerate((2, 1, 3)):
        xx = (x + k) % 4
        c = remote(csend.at[xx], crecv.at[x], cssem, crsem, at(z, y, xx))
        c.start()
        combine.append(c)
    for dev in lines:
        pl.semaphore_signal(ready.at[0], inc=1, device_id=dev, device_id_type=MESH)

    small = [
        remote(res_ref.at[pl.ds((1 - s) * 32, 32)], resin, smallsem.at[0], smallrs.at[0], other),
        remote(gain_ref, gainin, smallsem.at[1], smallrs.at[1], other),
    ]
    for c in small:
        c.start()
    sends = []
    for i, (c, src, dst) in enumerate(weights):
        c = remote(src, dst, wssem.at[i], wrsem.at[i], other)
        c.start()
        sends.append(c)

    def halves(own, theirs):
        first = jnp.where(s == 0, own, theirs)
        second = jnp.where(s == 0, theirs, own)
        return jnp.concatenate([first, second], axis=1)

    for c in small:
        c.wait_recv()
    stream[...] = halves(
        res_ref[pl.ds(s * 32, 32), :].astype(F32), resin[...].astype(F32)
    )
    gains[me] = halves(gain_ref[...], gainin[...])

    def gain_stage(j, start, count, devs):
        part = gains.at[pl.ds(start, count)]
        cs = []
        for dev in devs:
            c = remote(part, part, gssem.at[j], grsem.at[j], dev)
            c.start()
            cs.append(c)
        return cs

    def settle(sem, ref, send=False):
        c = remote(ref, ref, sem, sem, other)
        if send:
            c.wait_send()
        else:
            c.wait_recv()

    gain_stage(0, me, 1, lines[:3])
    pl.semaphore_wait(ready.at[0], 9)
    for dev in lines:
        pl.semaphore_signal(ready.at[1], inc=1, device_id=dev, device_id_type=MESH)

    settle(crsem, crecv.at[pl.ds(0, 3)])
    crecv[x] = csend[x]
    parts = []
    for i in range(4):
        code = crecv[i, 32:64, :].astype(F32)
        m = code[:, 0:1] + code[:, 1:2] + code[:, 2:3]
        d = code[:, 3:4] + code[:, 4:5]
        parts.append((m, d, crecv[i, 0:32, :].astype(F32)))
    peak = jnp.maximum(
        jnp.maximum(parts[0][0], parts[1][0]), jnp.maximum(parts[2][0], parts[3][0])
    )
    num, den = 0.0, 0.0
    for m, d, n in parts:
        f = jnp.exp(m - peak)
        num = num + n * f
        den = den + d * f
    ag1[me] = (num / den).astype(BF16)

    pl.semaphore_wait(ready.at[1], 9)

    order = (0, 2, 1, 3)
    arrival = (0, 1, 3, 2)

    def each(g, step):
        if g == 0:
            lax.fori_loop(0, 10, step, 0)
            lax.fori_loop(11, 16, step, 0)
        else:
            lax.fori_loop(0, 16, step, 0)

    def spread(buf, ssem, rsem, by):
        for g in order:
            def step(i, carry, g=g):
                a, b = (i // 4 + 2) % 4, (i + 2) % 4
                if by == "x":
                    dev = at((z + a) % 4, (y + b) % 4, (x + g) % 4)
                else:
                    dev = at((z + g) % 4, (y + a) % 4, (x + b) % 4)
                remote(buf.at[me], buf.at[me], ssem, rsem.at[g], dev).start()
                return carry
            each(g, step)

    spread(ag1, as1, ar1, "x")

    settle(grsem.at[0], gains.at[pl.ds(0, 3)])
    gain_stage(1, w * 4, 4, lines[3:6])

    weights[0][0].wait()
    sends[0].wait_recv()
    total = stream[...]
    for n, g in enumerate(arrival):
        settle(ar1.at[g], ag1.at[pl.ds(0, 15 if g == 0 else 16)])
        xx = (x + 4 - g) % 4
        turned = []
        for half in range(2):
            rows = jnp.concatenate([ag1[4 * (8 * half + j) + xx] for j in range(8)], 0)
            turned.append(dot_nn(perm[...], rows).astype(BF16))
        rows = jnp.concatenate(
            [
                jnp.concatenate([part[16 * h : 16 * h + 16] for part in turned], 0)
                for h in range(16)
            ],
            axis=1,
        )
        total = total + dot_nt(rows, ow[:, pl.ds(pl.multiple_of(xx * 2048, 2048), 2048)])
        if n == 1:
            settle(grsem.at[1], gains.at[pl.ds(0, 12)])
            gain_stage(2, z * 16, 16, lines[6:9])
    rounded = total.astype(BF16)
    ag2[me] = rounded

    spread(ag2, as2, ar2, "z")

    def mixed(a, b):
        m = pltpu.roll(jnp.where(low, b, a), 64, 1)
        return jnp.where(low, a, m), jnp.where(low, m, b)

    kept = rounded.astype(F32)
    turned = pltpu.roll(kept, 64, 1)
    kept, turned = kept[:, :64], turned[:, :64]
    fsend[...] = jnp.where(s == 0, turned, kept).astype(BF16)
    mine = jnp.where(s == 0, kept, turned)
    swap = remote(fsend, frecv, fs, fr, other)
    swap.start()

    settle(grsem.at[2], gains.at[pl.ds(0, 48)])
    for t in range(32):
        first, second = mixed(gains[2 * t], gains[2 * t + 1])
        gnat[:, HEAD * t : HEAD * (t + 1)] = jnp.concatenate([first, first], 0).astype(BF16)
        gnat[:, 4096 + HEAD * t : 4096 + HEAD * (t + 1)] = jnp.concatenate(
            [second, second], 0
        ).astype(BF16)
    for c, _, _ in weights[1:3]:
        c.wait()
    for c in sends[1:3]:
        c.wait_recv()

    squares = jnp.zeros((32, 32), F32)
    gate = jnp.zeros((32, 2 * UNITS), F32)
    up = jnp.zeros((32, 2 * UNITS), F32)
    for g in arrival:
        settle(ar2.at[g], ag2.at[pl.ds(0, 15 if g == 0 else 16)])
        zz = (z + 4 - g) % 4
        sides = [[], []]
        for t in range(8):
            c = zz * 16 + 2 * t
            for e, part in enumerate(mixed(ag2[c].astype(F32), ag2[c + 1].astype(F32))):
                sides[e].append(part.astype(BF16))
        for e in range(2):
            part = jnp.concatenate(sides[e], axis=1)
            squares = squares + dot_nt(part, part)
            lanes = pl.ds(pl.multiple_of(4096 * e + zz * 1024, 1024), 1024)
            row = gnat[:, lanes]
            part = part * jnp.concatenate([row, row], 0)
            gate = gate + dot_nt(part, gw[:, lanes])
            up = up + dot_nt(part, uw[:, lanes])
    diagonal = lax.broadcasted_iota(jnp.int32, (32, 32), 0) == lax.broadcasted_iota(
        jnp.int32, (32, 32), 1
    )
    squares = jnp.sum(jnp.where(diagonal, squares, 0.0), axis=1, keepdims=True)
    inverse = lax.rsqrt(squares / D + 1e-05)
    v = gate * inverse
    hidden = (v / (1.0 + jnp.exp(-v)) * (up * inverse)).astype(BF16)

    weights[3][0].wait()
    sends[3].wait_recv()
    for g in (2, 1, 3, 0):
        zz = (z + g) % 4
        at0 = pl.ds(pl.multiple_of(zz * 1024, 1024), 1024)
        at1 = pl.ds(pl.multiple_of(4096 + zz * 1024, 1024), 1024)
        first = dot_nn(hidden, dw[:, at0])
        second = dot_nn(hidden, dw[:, at1])
        for t in range(8):
            lanes = slice(HEAD * t, HEAD * (t + 1))
            for e, part in enumerate((first[:, lanes], second[:, lanes])):
                a, b = mixed(part[:16], part[16:])
                rsend[zz * 16 + 2 * t, e] = a.astype(BF16)
                rsend[zz * 16 + 2 * t + 1, e] = b.astype(BF16)

        def step(i, carry, zz=zz, g=g):
            yy, xx = (y + i // 4 + 2) % 4, (x + i + 2) % 4
            c = zz * 4 + yy
            for e in range(2):
                remote(
                    rsend.at[c * 4 + xx, e], rrecv.at[s, me], rss, rsr.at[g], (e, c, xx)
                ).start()
            return carry

        each(g, step)
    remote(rsend.at[me, 1 - s], rrecv.at[s, me], rss, rsr.at[0], other).start()
    rrecv[s, me] = rsend[me, s]

    swap.wait_recv()
    theirs = frecv[...].astype(F32)
    totals = [jnp.zeros((16, HEAD), F32), jnp.zeros((16, HEAD), F32)]
    for g in arrival:
        settle(rsr.at[g], rrecv.at[0, pl.ds(0, 31 if g == 0 else 32)])
        zz = (z + 4 - g) % 4
        for e in range(2):
            part = rrecv[e, zz * 16].astype(F32)
            for n in range(1, 16):
                part = part + rrecv[e, zz * 16 + n].astype(F32)
            totals[e] = totals[e] + part
    for e in range(2):
        part = jnp.concatenate([totals[e], pltpu.roll(totals[e], 64, 1)], 0)[:, :64]
        start = jnp.where(s == e, mine, theirs)
        out_ref[pl.ds(32 * e, 32), :] = (start + part).astype(BF16)

    settle(cssem, csend.at[pl.ds(0, 3)], True)
    for c in small + sends:
        c.wait_send()
    settle(gssem.at[0], gains.at[pl.ds(0, 3)], True)
    settle(gssem.at[1], gains.at[pl.ds(0, 12)], True)
    settle(gssem.at[2], gains.at[pl.ds(0, 48)], True)
    settle(as1, ag1.at[pl.ds(0, 63)], True)
    settle(as2, ag2.at[pl.ds(0, 63)], True)
    settle(rss, rsend.at[pl.ds(0, 63)], True)
    settle(rss, rsend.at[0, 0], True)
    swap.wait_send()


def on_device(
    queries, key_cache, value_cache, latest_key, latest_value, lengths,
    residual, o_weight, norm_gain, gate_weight, up_weight, down_weight,
):
    vmem = pl.BlockSpec(memory_space=pltpu.VMEM)
    hbm = pl.BlockSpec(memory_space=pltpu.HBM)
    dma = pltpu.SemaphoreType.DMA
    return pl.pallas_call(
        layer_kernel,
        out_shape=jax.ShapeDtypeStruct((64, 64), BF16),
        in_specs=[hbm] * 12,
        out_specs=vmem,
        scratch_shapes=[
            pltpu.VMEM((2, D), BF16),
            pltpu.VMEM((2, 1024), BF16),
            pltpu.VMEM((2, 1024), BF16),
            pltpu.SMEM((2,), jnp.int32),
            pltpu.VMEM((64, 64), BF16),
            pltpu.VMEM((64,), BF16),
            pltpu.VMEM((8, 64), F32),
            dma((6,)),
            pltpu.VMEM((2, SPAN, 1024), BF16),
            pltpu.VMEM((2, SPAN, 1024), BF16),
            pltpu.VMEM((128, D), BF16),
            pltpu.VMEM((2 * UNITS, D), BF16),
            pltpu.VMEM((2 * UNITS, D), BF16),
            pltpu.VMEM((2 * UNITS, D), BF16),
            pltpu.VMEM((128, HEAD), F32),
            pltpu.VMEM((32, HEAD), F32),
            pltpu.VMEM((4, 64, HEAD), BF16),
            pltpu.VMEM((4, 64, HEAD), BF16),
            pltpu.VMEM((64, 32, HEAD), BF16),
            pltpu.VMEM((256, 256), BF16),
            pltpu.VMEM((64, 32, HEAD), BF16),
            pltpu.VMEM((16, D), BF16),
            pltpu.VMEM((64, 2, 16, HEAD), BF16),
            pltpu.VMEM((2, 64, 16, HEAD), BF16),
            pltpu.VMEM((32, 64), BF16),
            pltpu.VMEM((8, 64), F32),
            pltpu.VMEM((32, HEAD), F32),
            pltpu.VMEM((64, 8, HEAD), F32),
            pltpu.VMEM((32, 64), BF16),
            pltpu.VMEM((32, 64), BF16),
            dma((4,)), dma((4,)), dma((4,)), dma((4,)), dma((2,)), dma((2,)),
            dma, dma, dma((3,)), dma((3,)),
            dma, dma((4,)), dma, dma((4,)), dma, dma((4,)), dma, dma,
            pltpu.SemaphoreType.REGULAR((2,)),
        ],
        compiler_params=pltpu.CompilerParams(
            collective_id=0, has_side_effects=True, vmem_limit_bytes=64 << 20
        ),
    )(
        queries, latest_key, latest_value, lengths, residual, norm_gain,
        key_cache, value_cache, o_weight.T, gate_weight.T, up_weight.T, down_weight,
    )


def solution(mesh):
    sessions = ("side", "wide")
    every = ("side", "wide", "narrow")
    return jax.shard_map(
        on_device,
        mesh=mesh,
        in_specs=(
            P(sessions, None),
            P(sessions, "narrow", None),
            P(sessions, "narrow", None),
            P(sessions, None),
            P(sessions, None),
            P(sessions),
            P(None, every),
            P(None, every),
            P(every),
            P(None, every),
            P(None, every),
            P(every, None),
        ),
        out_specs=P(None, every),
        check_vma=False,
    )
```

```python
import jax
import jax.numpy as jnp
from jax import lax
from jax.experimental import pallas as pl
from jax.experimental.pallas import tpu as pltpu
from jax.sharding import PartitionSpec as P

D = 8192
HEAD = 128
SPAN = 1024
UNITS = 224
SCALE = HEAD**-0.5
NEG = -1e30
MESH = pl.DeviceIdType.MESH
F32 = jnp.float32
BF16 = jnp.bfloat16
NT = (((1,), (1,)), ((), ()))


def dot_nt(a, b):
    return lax.dot_general(a, b, NT, preferred_element_type=F32)


def dot_nn(a, b):
    return jnp.dot(a, b, preferred_element_type=F32)


def layer_kernel(
    q_hbm, lk_hbm, lv_hbm, len_hbm, res_hbm, gain_hbm,
    k_hbm, v_hbm, o_hbm, g_hbm, u_hbm, d_hbm,
    out_ref,
    q_ref, lk_ref, lv_ref, len_ref, res_ref, gain1, gain_ref, insem,
    kv, vv, ow, gw, uw, dw,
    qrow, lrow, csend, crecv, ag1, perm, ag2, gnat, rsend, rrecv,
    resin, gainin, stream, gains, gainx, gainy, fsend, frecv,
    kvsem, wsem, wssem, wrsem, smallsem, smallrs,
    cssem, crsem, gssem, grsem, as1, ar1, as2, ar2, rss, rsr, fs, fr,
    ready,
):
    s = lax.axis_index("side")
    w = lax.axis_index("wide")
    x = lax.axis_index("narrow")
    z, y = w // 4, w % 4
    me = w * 4 + x
    other = (1 - s, w, x)

    def at(zz, yy, xx):
        return (s, zz * 4 + yy, xx)

    lines = [at(z, y, (x + k) % 4) for k in (1, 2, 3)]
    lines += [at(z, (y + k) % 4, x) for k in (1, 2, 3)]
    lines += [at((z + k) % 4, y, x) for k in (1, 2, 3)]

    def remote(src, dst, ssem, rsem, dev):
        return pltpu.make_async_remote_copy(
            src_ref=src, dst_ref=dst, send_sem=ssem, recv_sem=rsem,
            device_id=dev, device_id_type=MESH,
        )

    inputs = []
    for i, (src, dst) in enumerate(
        (
            (q_hbm, q_ref), (lk_hbm, lk_ref), (lv_hbm, lv_ref),
            (len_hbm, len_ref), (res_hbm, res_ref), (gain_hbm, gain1),
        )
    ):
        c = pltpu.make_async_copy(src, dst, insem.at[i])
        c.start()
        inputs.append(c)
    loads = []
    for i in range(2):
        for src, dst, j in ((k_hbm, kv, 0), (v_hbm, vv, 1)):
            c = pltpu.make_async_copy(src.at[i], dst.at[i], kvsem.at[2 * i + j])
            c.start()
            loads.append(c)
    barrier = pltpu.get_barrier_semaphore()
    for dev in lines + [other]:
        pl.semaphore_signal(barrier, inc=1, device_id=dev, device_id_type=MESH)
    for c in inputs:
        c.wait()
    gain_ref[...] = jnp.broadcast_to(gain1[...].astype(F32)[None, :], (8, 64))

    qf = q_ref[...].astype(F32)
    for h in range(64):
        qrow[pl.ds(h, 2, stride=64), :] = qf[:, h * HEAD : (h + 1) * HEAD]
    for j, ref in enumerate((lk_ref, lv_ref)):
        lf = ref[...].astype(F32)
        for g in range(8):
            lrow[pl.ds(16 * j + g, 2, stride=8), :] = lf[:, g * HEAD : (g + 1) * HEAD]

    lane = lax.broadcasted_iota(jnp.int32, (1, HEAD), 1)
    low = lane < 64
    positions = x * SPAN + lax.broadcasted_iota(jnp.int32, (1, SPAN), 1)
    zero8 = jnp.zeros((8, HEAD), F32)

    weights = []

    def fetch():
        for i, (src, dst, n) in enumerate(
            ((o_hbm, ow, 64), (g_hbm, gw, UNITS), (u_hbm, uw, UNITS), (d_hbm, dw, UNITS))
        ):
            dst = dst.at[pl.ds(s * n, n)]
            c = pltpu.make_async_copy(src, dst, wsem.at[i])
            c.start()
            weights.append((c, src, dst))

    def attend(i):
        valid = positions < len_ref[i]
        queries = [qrow[pl.ds(64 * i + 16 * p, 16), :] for p in range(4)]
        pairs = []
        for q16 in queries:
            pairs.append(
                jnp.concatenate(
                    [
                        jnp.concatenate([q16[:8], zero8], 1),
                        jnp.concatenate([zero8, q16[8:]], 1),
                    ],
                    0,
                ).astype(BF16)
            )

        def repeated(j):
            return jnp.concatenate(
                [
                    jnp.broadcast_to(lrow[pl.ds(16 * j + 8 * i + g, 1), :], (8, HEAD))
                    for g in range(8)
                ],
                0,
            )

        fresh = jnp.sum(jnp.concatenate(queries, 0) * repeated(0), axis=1, keepdims=True) * SCALE
        fresh = jnp.where(x == 0, fresh, NEG)
        loads[2 * i].wait()
        score = jnp.concatenate(
            [dot_nt(pairs[p], kv[i, :, 256 * p : 256 * (p + 1)]) for p in range(4)], 0
        )
        score = jnp.where(valid, score * SCALE, NEG)
        top = jnp.max(score, axis=1, keepdims=True)
        weight = jnp.where(valid, jnp.exp(score - top), 0.0)
        den = jnp.sum(weight, axis=1, keepdims=True)
        rounded = weight.astype(BF16)
        loads[2 * i + 1].wait()
        nums = []
        for p in range(4):
            both = dot_nn(rounded[16 * p : 16 * p + 16], vv[i, :, 256 * p : 256 * (p + 1)])
            nums += [both[:8, :HEAD], both[8:, HEAD:]]
        num = jnp.concatenate(nums, 0)
        peak = jnp.maximum(top, fresh)
        shrink = jnp.exp(top - peak)
        own = jnp.where(x == 0, jnp.exp(fresh - peak), 0.0)
        num = num * shrink + own * repeated(1)
        den = den * shrink + own
        m1 = peak.astype(BF16).astype(F32)
        m2 = (peak - m1).astype(BF16).astype(F32)
        m3 = (peak - m1) - m2
        d1 = den.astype(BF16).astype(F32)
        d2 = den - d1
        coded = jnp.where(
            lane == 0, m1,
            jnp.where(lane == 1, m2, jnp.where(lane == 2, m3, jnp.where(lane == 3, d1, d2))),
        )
        num, coded = num.astype(BF16), coded.astype(BF16)
        for p in range(4):
            csend[p, pl.ds(16 * i, 16), :] = num[16 * p : 16 * p + 16]
            csend[p, pl.ds(32 + 16 * i, 16), :] = coded[16 * p : 16 * p + 16]

    attend(0)
    fetch()
    attend(1)

    r = lax.broadcasted_iota(jnp.int32, (256, 256), 0)
    k = lax.broadcasted_iota(jnp.int32, (256, 256), 1)
    source = (r % 16 // 2) * 32 + (r % 2) * 16 + r // 16
    perm[...] = jnp.where(source == k, 1.0, 0.0).astype(BF16)

    pl.semaphore_wait(barrier, 10)
    combine = []
    for j, k in enumerate((2, 1, 3)):
        xx = (x + k) % 4
        c = remote(csend.at[xx], crecv.at[x], cssem, crsem, at(z, y, xx))
        c.start()
        combine.append(c)
    for dev in lines:
        pl.semaphore_signal(ready.at[0], inc=1, device_id=dev, device_id_type=MESH)

    small = [
        remote(res_ref.at[pl.ds((1 - s) * 32, 32)], resin, smallsem.at[0], smallrs.at[0], other),
        remote(gain_ref, gainin, smallsem.at[1], smallrs.at[1], other),
    ]
    for c in small:
        c.start()
    sends = []
    for i, (c, src, dst) in enumerate(weights):
        c = remote(src, dst, wssem.at[i], wrsem.at[i], other)
        c.start()
        sends.append(c)

    def halves(own, theirs):
        first = jnp.where(s == 0, own, theirs)
        second = jnp.where(s == 0, theirs, own)
        return jnp.concatenate([first, second], axis=1)

    for c in small:
        c.wait_recv()
    stream[...] = halves(
        res_ref[pl.ds(s * 32, 32), :].astype(F32), resin[...].astype(F32)
    )
    gainx[x] = halves(gain_ref[...], gainin[...])

    def gain_stage(j, part, devs):
        for dev in devs:
            remote(part, part, gssem.at[j], grsem.at[j], dev).start()

    def settle(sem, ref, send=False):
        c = remote(ref, ref, sem, sem, other)
        if send:
            c.wait_send()
        else:
            c.wait_recv()

    gain_stage(0, gainx.at[x], lines[:3])
    pl.semaphore_wait(ready.at[0], 9)
    for dev in lines:
        pl.semaphore_signal(ready.at[1], inc=1, device_id=dev, device_id_type=MESH)

    settle(crsem, crecv.at[pl.ds(0, 3)])
    crecv[x] = csend[x]
    parts = []
    for i in range(4):
        code = crecv[i, 32:64, :].astype(F32)
        m = code[:, 0:1] + code[:, 1:2] + code[:, 2:3]
        d = code[:, 3:4] + code[:, 4:5]
        parts.append((m, d, crecv[i, 0:32, :].astype(F32)))
    peak = jnp.maximum(
        jnp.maximum(parts[0][0], parts[1][0]), jnp.maximum(parts[2][0], parts[3][0])
    )
    num, den = 0.0, 0.0
    for m, d, n in parts:
        f = jnp.exp(m - peak)
        num = num + n * f
        den = den + d * f
    ag1[me] = (num / den).astype(BF16)

    pl.semaphore_wait(ready.at[1], 9)

    order = (0, 2, 1, 3)
    arrival = (0, 1, 3, 2)

    def each(g, step):
        if g == 0:
            lax.fori_loop(0, 10, step, 0)
            lax.fori_loop(11, 16, step, 0)
        else:
            lax.fori_loop(0, 16, step, 0)

    def spread(buf, ssem, rsem, by):
        for g in order if by == "x" else arrival:
            def step(i, carry, g=g):
                a, b = (i // 4 + 2) % 4, (i + 2) % 4
                if by == "x":
                    dev = at((z + a) % 4, (y + b) % 4, (x + g) % 4)
                else:
                    dev = at((z + g) % 4, (y + a) % 4, (x + b) % 4)
                remote(buf.at[me], buf.at[me], ssem, rsem.at[g], dev).start()
                return carry
            each(g, step)

    spread(ag1, as1, ar1, "x")

    settle(grsem.at[0], gainx.at[pl.ds(0, 3)])
    gainy[y] = jnp.concatenate([gainx[j][0:1] for j in range(4)] * 2, 0)
    gain_stage(1, gainy.at[y], lines[3:6])
    settle(grsem.at[1], gainy.at[pl.ds(0, 3)])
    plane = gains.at[pl.ds(z * 16, 16)]
    plane[...] = jnp.concatenate([gainy[j][0:4] for j in range(4)], 0)
    gain_stage(2, plane, lines[6:9])

    weights[0][0].wait()
    sends[0].wait_recv()
    total = stream[...]
    for n, g in enumerate(arrival):
        settle(ar1.at[g], ag1.at[pl.ds(0, 15 if g == 0 else 16)])
        xx = (x + 4 - g) % 4
        turned = []
        for half in range(2):
            rows = jnp.concatenate([ag1[4 * (8 * half + j) + xx] for j in range(8)], 0)
            turned.append(dot_nn(perm[...], rows).astype(BF16))
        rows = jnp.concatenate(
            [
                jnp.concatenate([part[16 * h : 16 * h + 16] for part in turned], 0)
                for h in range(16)
            ],
            axis=1,
        )
        total = total + dot_nt(rows, ow[:, pl.ds(pl.multiple_of(xx * 2048, 2048), 2048)])
    rounded = total.astype(BF16)
    ag2[me] = rounded

    spread(ag2, as2, ar2, "z")

    def mixed(a, b):
        m = pltpu.roll(jnp.where(low, b, a), 64, 1)
        return jnp.where(low, a, m), jnp.where(low, m, b)

    kept = rounded.astype(F32)
    turned = pltpu.roll(kept, 64, 1)
    kept, turned = kept[:, :64], turned[:, :64]
    fsend[...] = jnp.where(s == 0, turned, kept).astype(BF16)
    mine = jnp.where(s == 0, kept, turned)
    swap = remote(fsend, frecv, fs, fr, other)
    swap.start()

    settle(grsem.at[2], gains.at[pl.ds(0, 48)])
    evens = gains[pl.ds(0, 32, stride=2), :]
    odds = gains[pl.ds(1, 32, stride=2), :]
    for e, part in enumerate(mixed(evens, odds)):
        for t in range(32):
            gnat[:, 4096 * e + HEAD * t : 4096 * e + HEAD * (t + 1)] = jnp.broadcast_to(
                part[t : t + 1], (16, HEAD)
            ).astype(BF16)
    for c, _, _ in weights[1:3]:
        c.wait()
    for c in sends[1:3]:
        c.wait_recv()

    squares = jnp.zeros((32, 32), F32)
    gate = jnp.zeros((32, 2 * UNITS), F32)
    up = jnp.zeros((32, 2 * UNITS), F32)
    for g in arrival:
        settle(ar2.at[g], ag2.at[pl.ds(0, 15 if g == 0 else 16)])
        zz = (z + 4 - g) % 4
        sides = [[], []]
        for t in range(8):
            c = zz * 16 + 2 * t
            for e, part in enumerate(mixed(ag2[c].astype(F32), ag2[c + 1].astype(F32))):
                sides[e].append(part.astype(BF16))
        for e in range(2):
            part = jnp.concatenate(sides[e], axis=1)
            squares = squares + dot_nt(part, part)
            lanes = pl.ds(pl.multiple_of(4096 * e + zz * 1024, 1024), 1024)
            row = gnat[:, lanes]
            part = part * jnp.concatenate([row, row], 0)
            gate = gate + dot_nt(part, gw[:, lanes])
            up = up + dot_nt(part, uw[:, lanes])
    diagonal = lax.broadcasted_iota(jnp.int32, (32, 32), 0) == lax.broadcasted_iota(
        jnp.int32, (32, 32), 1
    )
    squares = jnp.sum(jnp.where(diagonal, squares, 0.0), axis=1, keepdims=True)
    inverse = lax.rsqrt(squares / D + 1e-05)
    v = gate * inverse
    hidden = (v / (1.0 + jnp.exp(-v)) * (up * inverse)).astype(BF16)

    weights[3][0].wait()
    sends[3].wait_recv()
    for g in (2, 1, 3, 0):
        zz = (z + g) % 4
        at0 = pl.ds(pl.multiple_of(zz * 1024, 1024), 1024)
        at1 = pl.ds(pl.multiple_of(4096 + zz * 1024, 1024), 1024)
        first = dot_nn(hidden, dw[:, at0])
        second = dot_nn(hidden, dw[:, at1])
        for t in range(8):
            lanes = slice(HEAD * t, HEAD * (t + 1))
            for e, part in enumerate((first[:, lanes], second[:, lanes])):
                a, b = mixed(part[:16], part[16:])
                rsend[zz * 16 + 2 * t, e] = a.astype(BF16)
                rsend[zz * 16 + 2 * t + 1, e] = b.astype(BF16)

        def step(i, carry, zz=zz, g=g):
            yy, xx = (y + i // 4 + 2) % 4, (x + i + 2) % 4
            c = zz * 4 + yy
            for e in range(2):
                remote(
                    rsend.at[c * 4 + xx, e], rrecv.at[s, me], rss, rsr.at[g], (e, c, xx)
                ).start()
            return carry

        each(g, step)
    remote(rsend.at[me, 1 - s], rrecv.at[s, me], rss, rsr.at[0], other).start()
    rrecv[s, me] = rsend[me, s]

    swap.wait_recv()
    theirs = frecv[...].astype(F32)
    totals = [jnp.zeros((16, HEAD), F32), jnp.zeros((16, HEAD), F32)]
    for g in arrival:
        settle(rsr.at[g], rrecv.at[0, pl.ds(0, 31 if g == 0 else 32)])
        zz = (z + 4 - g) % 4
        for e in range(2):
            part = rrecv[e, zz * 16].astype(F32)
            for n in range(1, 16):
                part = part + rrecv[e, zz * 16 + n].astype(F32)
            totals[e] = totals[e] + part
    for e in range(2):
        part = jnp.concatenate([totals[e], pltpu.roll(totals[e], 64, 1)], 0)[:, :64]
        start = jnp.where(s == e, mine, theirs)
        out_ref[pl.ds(32 * e, 32), :] = (start + part).astype(BF16)

    settle(cssem, csend.at[pl.ds(0, 3)], True)
    for c in small + sends:
        c.wait_send()
    settle(gssem.at[0], gainx.at[pl.ds(0, 3)], True)
    settle(gssem.at[1], gainy.at[pl.ds(0, 3)], True)
    settle(gssem.at[2], gains.at[pl.ds(0, 48)], True)
    settle(as1, ag1.at[pl.ds(0, 63)], True)
    settle(as2, ag2.at[pl.ds(0, 63)], True)
    settle(rss, rsend.at[pl.ds(0, 63)], True)
    settle(rss, rsend.at[0, 0], True)
    swap.wait_send()


def on_device(
    queries, key_cache, value_cache, latest_key, latest_value, lengths,
    residual, o_weight, norm_gain, gate_weight, up_weight, down_weight,
):
    vmem = pl.BlockSpec(memory_space=pltpu.VMEM)
    hbm = pl.BlockSpec(memory_space=pltpu.HBM)
    dma = pltpu.SemaphoreType.DMA
    return pl.pallas_call(
        layer_kernel,
        out_shape=jax.ShapeDtypeStruct((64, 64), BF16),
        in_specs=[hbm] * 12,
        out_specs=vmem,
        scratch_shapes=[
            pltpu.VMEM((2, D), BF16),
            pltpu.VMEM((2, 1024), BF16),
            pltpu.VMEM((2, 1024), BF16),
            pltpu.SMEM((2,), jnp.int32),
            pltpu.VMEM((64, 64), BF16),
            pltpu.VMEM((64,), BF16),
            pltpu.VMEM((8, 64), F32),
            dma((6,)),
            pltpu.VMEM((2, SPAN, 1024), BF16),
            pltpu.VMEM((2, SPAN, 1024), BF16),
            pltpu.VMEM((128, D), BF16),
            pltpu.VMEM((2 * UNITS, D), BF16),
            pltpu.VMEM((2 * UNITS, D), BF16),
            pltpu.VMEM((2 * UNITS, D), BF16),
            pltpu.VMEM((128, HEAD), F32),
            pltpu.VMEM((32, HEAD), F32),
            pltpu.VMEM((4, 64, HEAD), BF16),
            pltpu.VMEM((4, 64, HEAD), BF16),
            pltpu.VMEM((64, 32, HEAD), BF16),
            pltpu.VMEM((256, 256), BF16),
            pltpu.VMEM((64, 32, HEAD), BF16),
            pltpu.VMEM((16, D), BF16),
            pltpu.VMEM((64, 2, 16, HEAD), BF16),
            pltpu.VMEM((2, 64, 16, HEAD), BF16),
            pltpu.VMEM((32, 64), BF16),
            pltpu.VMEM((8, 64), F32),
            pltpu.VMEM((32, HEAD), F32),
            pltpu.VMEM((64, HEAD), F32),
            pltpu.VMEM((4, 8, HEAD), F32),
            pltpu.VMEM((4, 8, HEAD), F32),
            pltpu.VMEM((32, 64), BF16),
            pltpu.VMEM((32, 64), BF16),
            dma((4,)), dma((4,)), dma((4,)), dma((4,)), dma((2,)), dma((2,)),
            dma, dma, dma((3,)), dma((3,)),
            dma, dma((4,)), dma, dma((4,)), dma, dma((4,)), dma, dma,
            pltpu.SemaphoreType.REGULAR((2,)),
        ],
        compiler_params=pltpu.CompilerParams(
            collective_id=0, has_side_effects=True, vmem_limit_bytes=64 << 20
        ),
    )(
        queries, latest_key, latest_value, lengths, residual, norm_gain,
        key_cache, value_cache, o_weight.T, gate_weight.T, up_weight.T, down_weight,
    )


def solution(mesh):
    sessions = ("side", "wide")
    every = ("side", "wide", "narrow")
    return jax.shard_map(
        on_device,
        mesh=mesh,
        in_specs=(
            P(sessions, None),
            P(sessions, "narrow", None),
            P(sessions, "narrow", None),
            P(sessions, None),
            P(sessions, None),
            P(sessions),
            P(None, every),
            P(None, every),
            P(every),
            P(None, every),
            P(None, every),
            P(every, None),
        ),
        out_specs=P(None, every),
        check_vma=False,
    )
```

```python
import jax
import jax.numpy as jnp
from jax import lax
from jax.experimental import pallas as pl
from jax.experimental.pallas import tpu as pltpu
from jax.sharding import PartitionSpec as P

D = 8192
HEAD = 128
SPAN = 1024
UNITS = 224
SCALE = HEAD**-0.5
NEG = -1e30
MESH = pl.DeviceIdType.MESH
F32 = jnp.float32
BF16 = jnp.bfloat16
NT = (((1,), (1,)), ((), ()))


def dot_nt(a, b):
    return lax.dot_general(a, b, NT, preferred_element_type=F32)


def dot_nn(a, b):
    return jnp.dot(a, b, preferred_element_type=F32)


def layer_kernel(
    q_hbm, lk_hbm, lv_hbm, len_hbm, res_hbm, gain_hbm,
    k_hbm, v_hbm, o_hbm, g_hbm, u_hbm, d_hbm,
    out_ref,
    q_ref, lk_ref, lv_ref, len_ref, res_ref, gain1, gain_ref, insem,
    kv, vv, ow, gw, uw, dw,
    qrow, lrow, csend, crecv, ag1, perm, ag2, gnat, rsend, rrecv,
    resin, gainin, stream, gains, gainx, gainy, fsend, frecv,
    kvsem, wsem, wssem, wrsem, smallsem, smallrs,
    cssem, crsem, gssem, grsem, as1, ar1, as2, ar2, rss, rsr, fs, fr,
    ready,
):
    s = lax.axis_index("side")
    w = lax.axis_index("wide")
    x = lax.axis_index("narrow")
    z, y = w // 4, w % 4
    me = w * 4 + x
    other = (1 - s, w, x)

    def at(zz, yy, xx):
        return (s, zz * 4 + yy, xx)

    lines = [at(z, y, (x + k) % 4) for k in (1, 2, 3)]
    lines += [at(z, (y + k) % 4, x) for k in (1, 2, 3)]
    lines += [at((z + k) % 4, y, x) for k in (1, 2, 3)]

    def remote(src, dst, ssem, rsem, dev):
        return pltpu.make_async_remote_copy(
            src_ref=src, dst_ref=dst, send_sem=ssem, recv_sem=rsem,
            device_id=dev, device_id_type=MESH,
        )

    inputs = []
    for i, (src, dst) in enumerate(
        (
            (q_hbm, q_ref), (lk_hbm, lk_ref), (lv_hbm, lv_ref),
            (len_hbm, len_ref), (res_hbm, res_ref), (gain_hbm, gain1),
        )
    ):
        c = pltpu.make_async_copy(src, dst, insem.at[i])
        c.start()
        inputs.append(c)
    loads = []
    for i in range(2):
        for src, dst, j in ((k_hbm, kv, 0), (v_hbm, vv, 1)):
            c = pltpu.make_async_copy(src.at[i], dst.at[i], kvsem.at[2 * i + j])
            c.start()
            loads.append(c)
    barrier = pltpu.get_barrier_semaphore()
    for dev in lines + [other]:
        pl.semaphore_signal(barrier, inc=1, device_id=dev, device_id_type=MESH)
    for c in inputs:
        c.wait()
    gain_ref[...] = jnp.broadcast_to(gain1[...].astype(F32)[None, :], (8, 64))

    qf = q_ref[...].astype(F32)
    for h in range(64):
        qrow[pl.ds(h, 2, stride=64), :] = qf[:, h * HEAD : (h + 1) * HEAD]
    for j, ref in enumerate((lk_ref, lv_ref)):
        lf = ref[...].astype(F32)
        for g in range(8):
            lrow[pl.ds(16 * j + g, 2, stride=8), :] = lf[:, g * HEAD : (g + 1) * HEAD]

    lane = lax.broadcasted_iota(jnp.int32, (1, HEAD), 1)
    low = lane < 64
    positions = x * SPAN + lax.broadcasted_iota(jnp.int32, (1, SPAN), 1)
    zero8 = jnp.zeros((8, HEAD), F32)

    weights = []

    def fetch():
        for i, (src, dst, n) in enumerate(
            ((o_hbm, ow, 64), (g_hbm, gw, UNITS), (u_hbm, uw, UNITS), (d_hbm, dw, UNITS))
        ):
            dst = dst.at[pl.ds(s * n, n)]
            c = pltpu.make_async_copy(src, dst, wsem.at[i])
            c.start()
            weights.append((c, src, dst))

    def attend(i):
        valid = positions < len_ref[i]
        queries = [qrow[pl.ds(64 * i + 16 * p, 16), :] for p in range(4)]
        pairs = []
        for q16 in queries:
            pairs.append(
                jnp.concatenate(
                    [
                        jnp.concatenate([q16[:8], zero8], 1),
                        jnp.concatenate([zero8, q16[8:]], 1),
                    ],
                    0,
                ).astype(BF16)
            )

        def repeated(j):
            return jnp.concatenate(
                [
                    jnp.broadcast_to(lrow[pl.ds(16 * j + 8 * i + g, 1), :], (8, HEAD))
                    for g in range(8)
                ],
                0,
            )

        fresh = jnp.sum(jnp.concatenate(queries, 0) * repeated(0), axis=1, keepdims=True) * SCALE
        fresh = jnp.where(x == 0, fresh, NEG)
        loads[2 * i].wait()
        score = jnp.concatenate(
            [dot_nt(pairs[p], kv[i, :, 256 * p : 256 * (p + 1)]) for p in range(4)], 0
        )
        score = jnp.where(valid, score * SCALE, NEG)
        top = jnp.max(score, axis=1, keepdims=True)
        weight = jnp.where(valid, jnp.exp(score - top), 0.0)
        den = jnp.sum(weight, axis=1, keepdims=True)
        rounded = weight.astype(BF16)
        loads[2 * i + 1].wait()
        nums = []
        for p in range(4):
            both = dot_nn(rounded[16 * p : 16 * p + 16], vv[i, :, 256 * p : 256 * (p + 1)])
            nums += [both[:8, :HEAD], both[8:, HEAD:]]
        num = jnp.concatenate(nums, 0)
        peak = jnp.maximum(top, fresh)
        shrink = jnp.exp(top - peak)
        own = jnp.where(x == 0, jnp.exp(fresh - peak), 0.0)
        num = num * shrink + own * repeated(1)
        den = den * shrink + own
        m1 = peak.astype(BF16).astype(F32)
        m2 = (peak - m1).astype(BF16).astype(F32)
        m3 = (peak - m1) - m2
        d1 = den.astype(BF16).astype(F32)
        d2 = den - d1
        coded = jnp.where(
            lane == 0, m1,
            jnp.where(lane == 1, m2, jnp.where(lane == 2, m3, jnp.where(lane == 3, d1, d2))),
        )
        num, coded = num.astype(BF16), coded.astype(BF16)
        for p in range(4):
            csend[p, pl.ds(16 * i, 16), :] = num[16 * p : 16 * p + 16]
            csend[p, pl.ds(32 + 16 * i, 16), :] = coded[16 * p : 16 * p + 16]

    attend(0)
    fetch()
    attend(1)

    r = lax.broadcasted_iota(jnp.int32, (256, 256), 0)
    k = lax.broadcasted_iota(jnp.int32, (256, 256), 1)
    source = (r % 16 // 2) * 32 + (r % 2) * 16 + r // 16
    perm[...] = jnp.where(source == k, 1.0, 0.0).astype(BF16)

    pl.semaphore_wait(barrier, 10)
    combine = []
    for j, k in enumerate((2, 1, 3)):
        xx = (x + k) % 4
        c = remote(csend.at[xx], crecv.at[x], cssem, crsem, at(z, y, xx))
        c.start()
        combine.append(c)
    for dev in lines:
        pl.semaphore_signal(ready.at[0], inc=1, device_id=dev, device_id_type=MESH)

    small = [
        remote(res_ref.at[pl.ds((1 - s) * 32, 32)], resin, smallsem.at[0], smallrs.at[0], other),
        remote(gain_ref, gainin, smallsem.at[1], smallrs.at[1], other),
    ]
    for c in small:
        c.start()
    sends = []
    for i, (c, src, dst) in enumerate(weights):
        c = remote(src, dst, wssem.at[i], wrsem.at[i], other)
        c.start()
        sends.append(c)

    def halves(own, theirs):
        first = jnp.where(s == 0, own, theirs)
        second = jnp.where(s == 0, theirs, own)
        return jnp.concatenate([first, second], axis=1)

    for c in small:
        c.wait_recv()
    stream[...] = halves(
        res_ref[pl.ds(s * 32, 32), :].astype(F32), resin[...].astype(F32)
    )
    gainx[x] = halves(gain_ref[...], gainin[...])

    def gain_stage(j, part, devs):
        for dev in devs:
            remote(part, part, gssem.at[j], grsem.at[j], dev).start()

    def settle(sem, ref, send=False):
        c = remote(ref, ref, sem, sem, other)
        if send:
            c.wait_send()
        else:
            c.wait_recv()

    gain_stage(0, gainx.at[x], lines[:3])
    pl.semaphore_wait(ready.at[0], 9)
    for dev in lines:
        pl.semaphore_signal(ready.at[1], inc=1, device_id=dev, device_id_type=MESH)

    settle(crsem, crecv.at[pl.ds(0, 3)])
    crecv[x] = csend[x]
    parts = []
    for i in range(4):
        code = crecv[i, 32:64, :].astype(F32)
        m = code[:, 0:1] + code[:, 1:2] + code[:, 2:3]
        d = code[:, 3:4] + code[:, 4:5]
        parts.append((m, d, crecv[i, 0:32, :].astype(F32)))
    peak = jnp.maximum(
        jnp.maximum(parts[0][0], parts[1][0]), jnp.maximum(parts[2][0], parts[3][0])
    )
    num, den = 0.0, 0.0
    for m, d, n in parts:
        f = jnp.exp(m - peak)
        num = num + n * f
        den = den + d * f
    ag1[me] = (num / den).astype(BF16)

    pl.semaphore_wait(ready.at[1], 9)

    order = (0, 1, 3, 2)
    arrival = (0, 1, 3, 2)

    def each(g, step):
        if g == 0:
            lax.fori_loop(0, 10, step, 0)
            lax.fori_loop(11, 16, step, 0)
        else:
            lax.fori_loop(0, 16, step, 0)

    def spread(buf, ssem, rsem, by):
        for g in order if by == "x" else arrival:
            def step(i, carry, g=g):
                a, b = (i // 4 + 2) % 4, (i + 2) % 4
                if by == "x":
                    dev = at((z + a) % 4, (y + b) % 4, (x + g) % 4)
                else:
                    dev = at((z + g) % 4, (y + a) % 4, (x + b) % 4)
                remote(buf.at[me], buf.at[me], ssem, rsem.at[g], dev).start()
                return carry
            each(g, step)

    spread(ag1, as1, ar1, "x")

    settle(grsem.at[0], gainx.at[pl.ds(0, 3)])
    gainy[y] = jnp.concatenate([gainx[j][0:1] for j in range(4)] * 2, 0)
    gain_stage(1, gainy.at[y], lines[3:6])
    settle(grsem.at[1], gainy.at[pl.ds(0, 3)])
    plane = gains.at[pl.ds(z * 16, 16)]
    plane[...] = jnp.concatenate([gainy[j][0:4] for j in range(4)], 0)
    gain_stage(2, plane, lines[6:9])

    weights[0][0].wait()
    sends[0].wait_recv()
    total = stream[...]
    for n, g in enumerate(arrival):
        settle(ar1.at[g], ag1.at[pl.ds(0, 15 if g == 0 else 16)])
        xx = (x + 4 - g) % 4
        turned = []
        for half in range(2):
            rows = jnp.concatenate([ag1[4 * (8 * half + j) + xx] for j in range(8)], 0)
            turned.append(dot_nn(perm[...], rows).astype(BF16))
        rows = jnp.concatenate(
            [
                jnp.concatenate([part[16 * h : 16 * h + 16] for part in turned], 0)
                for h in range(16)
            ],
            axis=1,
        )
        total = total + dot_nt(rows, ow[:, pl.ds(pl.multiple_of(xx * 2048, 2048), 2048)])
    rounded = total.astype(BF16)
    ag2[me] = rounded

    spread(ag2, as2, ar2, "z")

    def mixed(a, b):
        m = pltpu.roll(jnp.where(low, b, a), 64, 1)
        return jnp.where(low, a, m), jnp.where(low, m, b)

    kept = rounded.astype(F32)
    turned = pltpu.roll(kept, 64, 1)
    kept, turned = kept[:, :64], turned[:, :64]
    fsend[...] = jnp.where(s == 0, turned, kept).astype(BF16)
    mine = jnp.where(s == 0, kept, turned)
    swap = remote(fsend, frecv, fs, fr, other)
    swap.start()

    settle(grsem.at[2], gains.at[pl.ds(0, 48)])
    evens = gains[pl.ds(0, 32, stride=2), :]
    odds = gains[pl.ds(1, 32, stride=2), :]
    for e, part in enumerate(mixed(evens, odds)):
        for t in range(32):
            gnat[:, 4096 * e + HEAD * t : 4096 * e + HEAD * (t + 1)] = jnp.broadcast_to(
                part[t : t + 1], (16, HEAD)
            ).astype(BF16)
    for c, _, _ in weights[1:3]:
        c.wait()
    for c in sends[1:3]:
        c.wait_recv()

    squares = jnp.zeros((32, 32), F32)
    gate = jnp.zeros((32, 2 * UNITS), F32)
    up = jnp.zeros((32, 2 * UNITS), F32)
    for g in arrival:
        settle(ar2.at[g], ag2.at[pl.ds(0, 15 if g == 0 else 16)])
        zz = (z + 4 - g) % 4
        sides = [[], []]
        for t in range(8):
            c = zz * 16 + 2 * t
            for e, part in enumerate(mixed(ag2[c].astype(F32), ag2[c + 1].astype(F32))):
                sides[e].append(part.astype(BF16))
        for e in range(2):
            part = jnp.concatenate(sides[e], axis=1)
            squares = squares + dot_nt(part, part)
            lanes = pl.ds(pl.multiple_of(4096 * e + zz * 1024, 1024), 1024)
            row = gnat[:, lanes]
            part = part * jnp.concatenate([row, row], 0)
            gate = gate + dot_nt(part, gw[:, lanes])
            up = up + dot_nt(part, uw[:, lanes])
    diagonal = lax.broadcasted_iota(jnp.int32, (32, 32), 0) == lax.broadcasted_iota(
        jnp.int32, (32, 32), 1
    )
    squares = jnp.sum(jnp.where(diagonal, squares, 0.0), axis=1, keepdims=True)
    inverse = lax.rsqrt(squares / D + 1e-05)
    v = gate * inverse
    hidden = (v / (1.0 + jnp.exp(-v)) * (up * inverse)).astype(BF16)

    weights[3][0].wait()
    sends[3].wait_recv()
    for g in (2, 1, 3, 0):
        zz = (z + g) % 4
        at0 = pl.ds(pl.multiple_of(zz * 1024, 1024), 1024)
        at1 = pl.ds(pl.multiple_of(4096 + zz * 1024, 1024), 1024)
        first = dot_nn(hidden, dw[:, at0])
        second = dot_nn(hidden, dw[:, at1])
        for t in range(8):
            lanes = slice(HEAD * t, HEAD * (t + 1))
            for e, part in enumerate((first[:, lanes], second[:, lanes])):
                a, b = mixed(part[:16], part[16:])
                rsend[zz * 16 + 2 * t, e] = a.astype(BF16)
                rsend[zz * 16 + 2 * t + 1, e] = b.astype(BF16)

        def step(i, carry, zz=zz, g=g):
            yy, xx = (y + i // 4 + 2) % 4, (x + i + 2) % 4
            c = zz * 4 + yy
            for e in range(2):
                remote(
                    rsend.at[c * 4 + xx, e], rrecv.at[s, me], rss, rsr.at[g], (e, c, xx)
                ).start()
            return carry

        each(g, step)
    remote(rsend.at[me, 1 - s], rrecv.at[s, me], rss, rsr.at[0], other).start()
    rrecv[s, me] = rsend[me, s]

    swap.wait_recv()
    theirs = frecv[...].astype(F32)
    totals = [jnp.zeros((16, HEAD), F32), jnp.zeros((16, HEAD), F32)]
    for g in arrival:
        settle(rsr.at[g], rrecv.at[0, pl.ds(0, 31 if g == 0 else 32)])
        zz = (z + 4 - g) % 4
        for e in range(2):
            part = rrecv[e, zz * 16].astype(F32)
            for n in range(1, 16):
                part = part + rrecv[e, zz * 16 + n].astype(F32)
            totals[e] = totals[e] + part
    for e in range(2):
        part = jnp.concatenate([totals[e], pltpu.roll(totals[e], 64, 1)], 0)[:, :64]
        start = jnp.where(s == e, mine, theirs)
        out_ref[pl.ds(32 * e, 32), :] = (start + part).astype(BF16)

    settle(cssem, csend.at[pl.ds(0, 3)], True)
    for c in small + sends:
        c.wait_send()
    settle(gssem.at[0], gainx.at[pl.ds(0, 3)], True)
    settle(gssem.at[1], gainy.at[pl.ds(0, 3)], True)
    settle(gssem.at[2], gains.at[pl.ds(0, 48)], True)
    settle(as1, ag1.at[pl.ds(0, 63)], True)
    settle(as2, ag2.at[pl.ds(0, 63)], True)
    settle(rss, rsend.at[pl.ds(0, 63)], True)
    settle(rss, rsend.at[0, 0], True)
    swap.wait_send()


def on_device(
    queries, key_cache, value_cache, latest_key, latest_value, lengths,
    residual, o_weight, norm_gain, gate_weight, up_weight, down_weight,
):
    vmem = pl.BlockSpec(memory_space=pltpu.VMEM)
    hbm = pl.BlockSpec(memory_space=pltpu.HBM)
    dma = pltpu.SemaphoreType.DMA
    return pl.pallas_call(
        layer_kernel,
        out_shape=jax.ShapeDtypeStruct((64, 64), BF16),
        in_specs=[hbm] * 12,
        out_specs=vmem,
        scratch_shapes=[
            pltpu.VMEM((2, D), BF16),
            pltpu.VMEM((2, 1024), BF16),
            pltpu.VMEM((2, 1024), BF16),
            pltpu.SMEM((2,), jnp.int32),
            pltpu.VMEM((64, 64), BF16),
            pltpu.VMEM((64,), BF16),
            pltpu.VMEM((8, 64), F32),
            dma((6,)),
            pltpu.VMEM((2, SPAN, 1024), BF16),
            pltpu.VMEM((2, SPAN, 1024), BF16),
            pltpu.VMEM((128, D), BF16),
            pltpu.VMEM((2 * UNITS, D), BF16),
            pltpu.VMEM((2 * UNITS, D), BF16),
            pltpu.VMEM((2 * UNITS, D), BF16),
            pltpu.VMEM((128, HEAD), F32),
            pltpu.VMEM((32, HEAD), F32),
            pltpu.VMEM((4, 64, HEAD), BF16),
            pltpu.VMEM((4, 64, HEAD), BF16),
            pltpu.VMEM((64, 32, HEAD), BF16),
            pltpu.VMEM((256, 256), BF16),
            pltpu.VMEM((64, 32, HEAD), BF16),
            pltpu.VMEM((16, D), BF16),
            pltpu.VMEM((64, 2, 16, HEAD), BF16),
            pltpu.VMEM((2, 64, 16, HEAD), BF16),
            pltpu.VMEM((32, 64), BF16),
            pltpu.VMEM((8, 64), F32),
            pltpu.VMEM((32, HEAD), F32),
            pltpu.VMEM((64, HEAD), F32),
            pltpu.VMEM((4, 8, HEAD), F32),
            pltpu.VMEM((4, 8, HEAD), F32),
            pltpu.VMEM((32, 64), BF16),
            pltpu.VMEM((32, 64), BF16),
            dma((4,)), dma((4,)), dma((4,)), dma((4,)), dma((2,)), dma((2,)),
            dma, dma, dma((3,)), dma((3,)),
            dma, dma((4,)), dma, dma((4,)), dma, dma((4,)), dma, dma,
            pltpu.SemaphoreType.REGULAR((2,)),
        ],
        compiler_params=pltpu.CompilerParams(
            collective_id=0, has_side_effects=True, vmem_limit_bytes=64 << 20
        ),
    )(
        queries, latest_key, latest_value, lengths, residual, norm_gain,
        key_cache, value_cache, o_weight.T, gate_weight.T, up_weight.T, down_weight,
    )


def solution(mesh):
    sessions = ("side", "wide")
    every = ("side", "wide", "narrow")
    return jax.shard_map(
        on_device,
        mesh=mesh,
        in_specs=(
            P(sessions, None),
            P(sessions, "narrow", None),
            P(sessions, "narrow", None),
            P(sessions, None),
            P(sessions, None),
            P(sessions),
            P(None, every),
            P(None, every),
            P(every),
            P(None, every),
            P(None, every),
            P(every, None),
        ),
        out_specs=P(None, every),
        check_vma=False,
    )
```
